32 devices in a mesh: items: 8 (over z, y), blk: 4 (over x, core).
Axes of the slice: x: 2, y: 2, z: 4, core: 2. Of those that a mesh axis runs over, the one named last changes fastest.
Arguments:
- block_input: bfloat16 [64, 4, 128, 768], P('items', 'blk'), may hold values from -6 to 6
- block_cotangent: bfloat16 [64, 4, 128, 768], P('items', 'blk'), may hold values from -6 to 6
- task_counts: int32 [64], P('items'), may hold values from 1 to 128, as said below
- group_mask: int32 [64, 4, 4], P('items'), may hold values from 0 to 1, as said below
- weight_qkv: float32 [768, 2304], P('items'), may hold values from -0.21875 to 0.21875
- weight_out: float32 [768, 768], P('items'), may hold values from -1.75 to 1.75
- weight_up: float32 [768, 3072], P('items'), may hold values from -0.21875 to 0.21875
- weight_down: float32 [3072, 768], P('items'), may hold values from -0.109375 to 0.109375
- vectors: float32 [12, 768], P(None, 'items'), may hold values from -1.2 to 1.4
- first_qkv: float32 [768, 2304], P('items'), may hold values from -80 to 80
- first_out: float32 [768, 768], P('items'), may hold values from -12 to 12
- first_up: float32 [768, 3072], P('items'), may hold values from -40 to 40
- first_down: float32 [3072, 768], P('items'), may hold values from -80 to 80
- first_vectors: float32 [12, 768], P(None, 'items'), may hold values from -128 to 128
- second_qkv: float32 [768, 2304], P('items'), may hold values from 8192 to 131072
- second_out: float32 [768, 768], P('items'), may hold values from 163.84 to 2621.44
- second_up: float32 [768, 3072], P('items'), may hold values from 1638.4 to 26214.4
- second_down: float32 [3072, 768], P('items'), may hold values from 6553.6 to 104857.6
- second_vectors: float32 [12, 768], P(None, 'items'), may hold values from 16384 to 262144
Outputs:
- block_output: bfloat16 [64, 4, 128, 768], P('items', 'blk')
- input_grad: float32 [64, 4, 128, 768], P('items', 'blk')
- new_weight_qkv: float32 [768, 2304], P('items')
- new_weight_out: float32 [768, 768], P('items')
- new_weight_up: float32 [768, 3072], P('items')
- new_weight_down: float32 [3072, 768], P('items')
- new_vectors: float32 [12, 768], P(None, 'items')
- new_first_qkv: float32 [768, 2304], P('items')
- new_first_out: float32 [768, 768], P('items')
- new_first_up: float32 [768, 3072], P('items')
- new_first_down: float32 [3072, 768], P('items')
- new_first_vectors: float32 [12, 768], P(None, 'items')
- new_second_qkv: float32 [768, 2304], P('items')
- new_second_out: float32 [768, 768], P('items')
- new_second_up: float32 [768, 3072], P('items')
- new_second_down: float32 [3072, 768], P('items')
- new_second_vectors: float32 [12, 768], P(None, 'items')
The draws below stay inside these ranges and needn't reach their ends.
Inputs may be any that keep to these rules, and one draw needn't show every extreme that they name: `task_counts`: among the 8 items of each index of items, one has exactly 128 valid task tokens. group_mask[item, q, k] is 1 for k = q and 0 for k > q; among the 8 items of each index of items, one has ones everywhere on and below the diagonal.
All inputs are finite; a program needn't handle non-finite values.
Results may differ from the reference program's by a relative error of at most 0.012.
The reference program's roundings to bfloat16 on the way count: a program that leaves them out, or rounds other values in their place, can miss the bound.
Values may be sent and summed in bfloat16 or wider, within the bound.
A program may use at most 256 MiB of HBM per device.

```python
import math
import jax
import jax.numpy as jnp
from jax import lax

D = 768
H = 12
HD = 64
FF = 3072
GROUPS = 4
GROUP = 128
ITEMS_DEV = 8
VECS = 12
STEP = 5
ITEMS = 64
TOKENS = 32768


def full_item(key):
    pick = jax.random.randint(key, (ITEMS // ITEMS_DEV,), 0, ITEMS_DEV)
    return jnp.arange(ITEMS) % ITEMS_DEV == jnp.repeat(pick, ITEMS_DEV)


def draw_task_counts(key, part):
    key = jax.random.fold_in(key, 11)
    one, two = jax.random.split(key)
    counts = jax.random.randint(one, (ITEMS,), 1, GROUP + 1)
    return jnp.where(full_item(two), GROUP, counts).astype(jnp.int32)


def draw_group_mask(key, part):
    key = jax.random.fold_in(key, 23)
    one, two = jax.random.split(key)
    bits = jax.random.randint(one, (ITEMS, GROUPS, GROUPS), 0, 2)
    rows = jnp.arange(GROUPS)[:, None]
    cols = jnp.arange(GROUPS)[None, :]
    below = (cols < rows)[None]
    filled = full_item(two)[:, None, None]
    lower = jnp.where(filled, 1, bits)
    mask = jnp.where((cols == rows)[None], 1, jnp.where(below, lower, 0))
    return mask.astype(jnp.int32)


def draw_vectors(key, part):
    key = jax.random.fold_in(key, 37)
    one, two = jax.random.split(key)
    level = jax.random.uniform(one, (VECS, D), jnp.float32, 0.6, 1.4)
    spread = jnp.clip(0.3 * jax.random.normal(two, (VECS, D), jnp.float32), -1.2, 1.2)
    row = jnp.arange(VECS)[:, None]
    return jnp.where((row == 0) | (row == 2), level, spread)


def block_levels(rng, dims, cuts, low, high):
    factor_of, own = 1.0, jax.random.fold_in(rng, 6)
    for dim, parts in cuts:
        steps = jnp.exp(jax.random.uniform(jax.random.fold_in(own, dim), (parts,), jnp.float32, low / len(cuts), high / len(cuts)))
        factor_of = factor_of * jnp.repeat(steps, dims[dim] // parts).reshape([-1 if axis == dim else 1 for axis in range(len(dims))])
    return factor_of


def noise(rng, shape, deviation, bound, cuts=(), kind=jnp.bfloat16):
    array = jax.random.normal(rng, shape, jnp.float32) * deviation
    if len(cuts) > 0:
        array = block_levels(rng, shape, cuts, -0.22, 0.18) * array
    return jnp.clip(array, min=-bound, max=bound).astype(kind)


def setup_inputs(seed: int = 0) -> dict:
    arg_keys = jax.random.split(jax.random.key(seed), 20)
    block_input = noise(arg_keys[0], (ITEMS, GROUPS, GROUP, D), 1.0, 6.0, ((0, 8), (1, 4)))
    block_cotangent = noise(arg_keys[1], (ITEMS, GROUPS, GROUP, D), 1.0, 6.0, ((0, 8), (1, 4)))
    task_counts = draw_task_counts(jax.random.fold_in(arg_keys[19], 71), 0)
    group_mask = draw_group_mask(jax.random.fold_in(arg_keys[19], 71), 0)
    weight_qkv = noise(arg_keys[4], (D, 3 * D), D ** -0.5, 0.21875, ((0, 8),), jnp.float32)
    weight_out = noise(arg_keys[5], (D, D), (D // 64) ** -0.5, 1.75, ((0, 8),), jnp.float32)
    weight_up = noise(arg_keys[6], (D, FF), D ** -0.5, 0.21875, ((0, 8),), jnp.float32)
    weight_down = noise(arg_keys[7], (FF, D), FF ** -0.5, 0.109375, ((0, 8),), jnp.float32)
    vectors = draw_vectors(jax.random.fold_in(arg_keys[19], 71), 0)
    first_qkv = noise(arg_keys[9], (D, 3 * D), (0.08 * TOKENS ** 0.5), 80.0, ((0, 8),), jnp.float32)
    first_out = noise(arg_keys[10], (D, D), (0.011 * TOKENS ** 0.5), 12.0, ((0, 8),), jnp.float32)
    first_up = noise(arg_keys[11], (D, FF), (0.035 * TOKENS ** 0.5), 40.0, ((0, 8),), jnp.float32)
    first_down = noise(arg_keys[12], (FF, D), (0.07 * TOKENS ** 0.5), 80.0, ((0, 8),), jnp.float32)
    first_vectors = noise(arg_keys[13], (VECS, D), (0.11 * TOKENS ** 0.5), 128.0, ((1, 8),), jnp.float32)
    second_qkv = jnp.clip(jnp.exp(math.log(131072.0) - 2.7725887 * jax.random.uniform(arg_keys[14], (D, 3 * D), jnp.float32) ** block_levels(arg_keys[14], (D, 3 * D), ((0, 8),), -0.2, 0.2)), 8192.0, 131072.0)
    second_out = jnp.clip(jnp.exp(math.log(2621.44) - 2.7725887 * jax.random.uniform(arg_keys[15], (D, D), jnp.float32) ** block_levels(arg_keys[15], (D, D), ((0, 8),), -0.2, 0.2)), 163.84, 2621.44)
    second_up = jnp.clip(jnp.exp(math.log(26214.4) - 2.7725887 * jax.random.uniform(arg_keys[16], (D, FF), jnp.float32) ** block_levels(arg_keys[16], (D, FF), ((0, 8),), -0.2, 0.2)), 1638.4, 26214.4)
    second_down = jnp.clip(jnp.exp(math.log(104857.6) - 2.7725887 * jax.random.uniform(arg_keys[17], (FF, D), jnp.float32) ** block_levels(arg_keys[17], (FF, D), ((0, 8),), -0.2, 0.2)), 6553.6, 104857.6)
    second_vectors = jnp.clip(jnp.exp(math.log(262144.0) - 2.7725887 * jax.random.uniform(arg_keys[18], (VECS, D), jnp.float32) ** block_levels(arg_keys[18], (VECS, D), ((1, 8),), -0.2, 0.2)), 16384.0, 262144.0)
    return {"block_input": block_input, "block_cotangent": block_cotangent, "task_counts": task_counts, "group_mask": group_mask, "weight_qkv": weight_qkv, "weight_out": weight_out, "weight_up": weight_up, "weight_down": weight_down, "vectors": vectors, "first_qkv": first_qkv, "first_out": first_out, "first_up": first_up, "first_down": first_down, "first_vectors": first_vectors, "second_qkv": second_qkv, "second_out": second_out, "second_up": second_up, "second_down": second_down, "second_vectors": second_vectors}


@jax.custom_vjp
def low(v):
    return lax.optimization_barrier(v.astype(jnp.bfloat16)).astype(jnp.float32)

@jax.custom_vjp
def low_back(v):
    return v

def low_keep(v):
    return (low(v), None)

def low_pass(kept, grad):
    return (grad,)

def back_keep(v):
    return (v, None)

def back_low(kept, grad):
    return (low(grad),)
low.defvjp(low_keep, low_pass)
low_back.defvjp(back_keep, back_low)
norm_eps = 1e-06
beta_one = 0.9
beta_two = 0.5
adam_eps = 1e-08
weight_decay = 0.1
rates = (0.1, 0.8, 0.1, 0.06, 1.0)
highest = lax.Precision.HIGHEST

def layer_norm(values, gain, shift):
    mean = lax.optimization_barrier(jnp.mean(values, -1, keepdims=True))
    centred = values - mean
    variance = lax.optimization_barrier(jnp.mean(centred * centred, -1, keepdims=True))
    return centred * lax.rsqrt(variance + norm_eps) * gain + shift

def key_mask(counts, masks):
    group_of = jnp.arange(GROUPS * GROUP, dtype=jnp.int32) // GROUP
    place = jnp.arange(GROUPS * GROUP, dtype=jnp.int32) % GROUP
    paired = masks[:, group_of, :][:, :, group_of]
    counted = (place[None, :] < counts[:, None]) | (group_of[None, :] > 0)
    return (paired > 0) & counted[:, None, :]

def block_forward(params, inputs, counts, masks):
    wqkv, wout, wup, wdown, vecs = params
    nitems = inputs.shape[0]
    length = GROUPS * GROUP
    seq = inputs.reshape(nitems, length, D)
    first = low(layer_norm(seq, vecs[0], vecs[1]))
    proj = jnp.einsum('bsd,de->bse', first, wqkv, precision=highest)
    bias = jnp.concatenate([vecs[4], jnp.zeros((D,), jnp.float32), vecs[5]])
    proj = low(low_back(proj + bias))
    query = proj[..., :D].reshape(nitems, length, H, HD)
    keyed = proj[..., D:2 * D].reshape(nitems, length, H, HD)
    valued = proj[..., 2 * D:].reshape(nitems, length, H, HD)
    scores = low_back(jnp.einsum('bihd,bjhd->bhij', query, keyed, precision=highest) * 0.125)
    allowed = key_mask(counts, masks)[:, None]
    scores = jnp.where(allowed, scores, -1e+30)
    top = lax.optimization_barrier(jnp.max(scores, -1, keepdims=True))
    raw = jnp.where(allowed, jnp.exp(scores - top), 0.0)
    probs = low(raw / lax.optimization_barrier(jnp.sum(raw, -1, keepdims=True)))
    mixed = jnp.einsum('bhij,bjhd->bihd', probs, valued, precision=highest).reshape(nitems, length, D)
    mixed = low(low_back(mixed))
    second_in = seq + low_back(jnp.einsum('bsd,de->bse', mixed, wout, precision=highest)) + vecs[6]
    second = low(layer_norm(second_in, vecs[2], vecs[3]))
    hidden = jnp.einsum('bsd,df->bsf', second, wup, precision=highest) + vecs[8:].reshape(FF)
    hidden = low_back(hidden)
    gelu_out = low(jax.nn.gelu(hidden, approximate=True))
    output = second_in + jnp.einsum('bsf,fd->bsd', gelu_out, wdown, precision=highest) + vecs[7]
    return output.reshape(inputs.shape)

def adamw(weight, first, second, grad, rate, decay_rate):
    first_new = beta_one * first + (1.0 - beta_one) * grad
    second_new = beta_two * second + (1.0 - beta_two) * grad * grad
    first_hat = first_new / (1.0 - beta_one ** STEP)
    second_hat = second_new / (1.0 - beta_two ** STEP)
    weight_new = weight - rate * (first_hat / (jnp.sqrt(second_hat) + adam_eps) + decay_rate * weight)
    return (weight_new, first_new, second_new)

def reference(block_input, block_cotangent, task_counts, group_mask, weight_qkv, weight_out, weight_up, weight_down, vectors, first_qkv, first_out, first_up, first_down, first_vectors, second_qkv, second_out, second_up, second_down, second_vectors):
    params = (weight_qkv, weight_out, weight_up, weight_down, vectors)
    inputs = block_input.astype(jnp.float32)
    block_items = math.gcd(ITEMS, 8)
    nblocks = ITEMS // block_items

    def full(params, inputs):
        lows = tuple((low(p) for p in params))

        def step(carry, block):
            return (carry, jax.checkpoint(block_forward)(lows, block[0], block[1], block[2]))
        blocks = (inputs.reshape(nblocks, block_items, GROUPS, GROUP, D), task_counts.reshape(nblocks, block_items), group_mask.reshape(nblocks, block_items, GROUPS, GROUPS))
        _, outputs = lax.scan(step, jnp.zeros((), jnp.float32), blocks)
        return outputs.reshape(inputs.shape)
    output, pull = jax.vjp(full, params, inputs)
    grads, input_grad = pull(block_cotangent.astype(jnp.float32))
    firsts = (first_qkv, first_out, first_up, first_down, first_vectors)
    seconds = (second_qkv, second_out, second_up, second_down, second_vectors)
    decays = (weight_decay, weight_decay, weight_decay, weight_decay, 0.0)
    updated = [adamw(params[n], firsts[n], seconds[n], grads[n], rates[n], decays[n]) for n in range(5)]
    return (output.astype(jnp.bfloat16), input_grad, updated[0][0], updated[1][0], updated[2][0], updated[3][0], updated[4][0], updated[0][1], updated[1][1], updated[2][1], updated[3][1], updated[4][1], updated[0][2], updated[1][2], updated[2][2], updated[3][2], updated[4][2])
```

```python
import collections

import jax
import jax.numpy as jnp
from jax import lax
from jax.experimental import pallas as pl
from jax.experimental.pallas import tpu as pltpu
from jax.sharding import PartitionSpec as P

D = 768
H = 12
HD = 64
FF = 3072
GROUPS = 4
GROUP = 128
STEP = 5
CHUNKS = 3
WIDE = 1024
VROWS = 16
OWNERS = 8
MIB = 1024 * 1024

norm_eps = 1e-06
beta_one = 0.9
beta_two = 0.5
adam_eps = 1e-08
weight_decay = 0.1
rates = (0.1, 0.8, 0.1, 0.06, 1.0)
decays = (weight_decay, weight_decay, weight_decay, weight_decay, 0.0)
masked_value = -1e30

bf = jnp.bfloat16
f32 = jnp.float32
MESH = pl.DeviceIdType.MESH
ANY = pl.BlockSpec(memory_space=pl.ANY)
VMEM = pl.BlockSpec(memory_space=pltpu.VMEM)
SMEM = pl.BlockSpec(memory_space=pltpu.SMEM)
TOKENS = (GROUPS, 2, GROUP, D)


def adamw(weight, first, second, grad, rate, decay_rate):
    first_new = beta_one * first + (1.0 - beta_one) * grad
    second_new = beta_two * second + (1.0 - beta_two) * grad * grad
    first_hat = first_new * (1.0 / (1.0 - beta_one**STEP))
    second_hat = second_new * (1.0 / (1.0 - beta_two**STEP))
    weight_new = weight - rate * (
        first_hat / (jnp.sqrt(second_hat) + adam_eps) + decay_rate * weight
    )
    return (weight_new, first_new, second_new)


def nn(a, b):
    return jnp.dot(a, b, preferred_element_type=f32)


def nt(a, b):
    return lax.dot_general(a, b, (((1,), (1,)), ((), ())), preferred_element_type=f32)


def tn(a, b):
    return lax.dot_general(a, b, (((0,), (0,)), ((), ())), preferred_element_type=f32)


def normal(values):
    mean = jnp.mean(values, -1, keepdims=True)
    centred = values - mean
    scale = lax.rsqrt(jnp.mean(centred * centred, -1, keepdims=True) + norm_eps)
    return centred * scale, scale


def norm_back(grad, normed, scale, gain):
    e = grad * gain
    along = jnp.mean(e * normed, -1, keepdims=True)
    return scale * (e - jnp.mean(e, -1, keepdims=True) - normed * along)


def rows_of(ref, g):
    block = ref[g]
    return block.reshape(2 * GROUP, block.shape[-1])


def halves(ref, k):
    block = ref[2 * k : 2 * k + 2]
    return block.reshape(512, block.shape[-1])


def put_rows(ref, g, values):
    ref[g] = values.reshape(2, GROUP, values.shape[-1])


def span256(g):
    return pl.ds(pl.multiple_of(g * 256, 256), 256)


def col_sum(values):
    return jnp.sum(values, 0, keepdims=True)


def stacked(pair, low):
    zero = jnp.zeros_like(pair)
    return jnp.concatenate([jnp.where(low, pair, zero), jnp.where(low, zero, pair)], 0)


def run_hooks(hooks, index):
    for at, hook in hooks.items():
        pl.when(index == at)(hook)


def up_block(c, i):
    lane = 3 * (i % 2) + c
    return slice(8 + i // 2, 9 + i // 2), slice(lane * 128, (lane + 1) * 128)


LAYER_BUFFERS = dict(
    x=(TOKENS, bf),
    dy=(TOKENS, bf),
    qkv=(TOKENS[:3] + (3 * D,), bf),
    o=(TOKENS, bf),
    x2=(TOKENS, f32),
    a2=(TOKENS, bf),
    a2t=((D, 1024), bf),
    dyt=((D, 1024), bf),
    gl=((1024, WIDE), bf),
    du=((1024, WIDE), bf),
    yacc=(TOKENS, f32),
    da2=(TOKENS, f32),
    dkv=((2, GROUPS * GROUP, 128), f32),
    eye=((256, 256), bf),
    stats=((H, GROUPS, 256), f32),
    vec=((VROWS, D), f32),
    bu=((CHUNKS, 1, WIDE), f32),
    gbu=((CHUNKS, 1, WIDE), f32),
    bqkv=((3, 1, D), f32),
    gv=((VROWS, D), f32),
    wqkv=((3, 4, 2, 2, 48, D), bf),
    wo=((4, 2, 2, 48, D), bf),
    wup=((CHUNKS, 4, 2, 2, 48, WIDE), bf),
    wdn=((CHUNKS, 4, 2, 2, 64, D), bf),
    gdn=((CHUNKS, 4, 2, 2, 384, 128), bf),
)


class Masks:
    def __init__(self, counts, masks):
        self.counts, self.masks, self.first = counts, masks, lax.axis_index("blk") * 2
        self.place = lax.broadcasted_iota(jnp.int32, (GROUP, 256), 0)

    def __call__(self, s, t, g):
        item = self.first + t
        open_first = self.masks[g, 0, item] * self.counts[item]
        parts = [jnp.where(self.place < open_first, s[:GROUP], masked_value)]
        for k in range(1, g + 1):
            part = s[k * GROUP : (k + 1) * GROUP]
            if k < g:
                part = part + (self.masks[g, k, item] - 1).astype(f32) * -masked_value
            parts.append(part)
        return jnp.concatenate(parts, 0)


class Layer:
    def __init__(self, refs, masks):
        self.r, self.masks = refs, masks
        self.low = lax.broadcasted_iota(jnp.int32, (1, 2 * HD), 1) < HD
        self.upper = lax.broadcasted_iota(jnp.int32, (2 * HD, 1), 0) < HD

    def start(self):
        r = self.r
        row = lax.broadcasted_iota(jnp.int32, (256, 256), 0)
        col = lax.broadcasted_iota(jnp.int32, (256, 256), 1)
        r.eye[...] = jnp.where(row == col, 1.0, 0.0).astype(bf)
        r.gv[...] = jnp.zeros_like(r.gv)
        r.gbu[...] = jnp.zeros_like(r.gbu)

    def turned(self, values):
        n = values.shape[1]
        return nt(self.r.eye[:n, :n], values).astype(bf)

    def turn_rows(self, ref, g, values):
        for m in range(3):
            ref[m * 256 : (m + 1) * 256, span256(g)] = self.turned(values[:, m * 256 : (m + 1) * 256])

    def own_heads(self, pair):
        return self.turned(jnp.where(self.upper, pair[:, :GROUP], pair[:, GROUP:]).astype(bf)).astype(bf)

    def qkv_grad(self, hq):
        return self.r.wdn.at[hq, :, :, :, pl.ds(0, 48), :]

    def vec(self, k):
        return self.r.vec[k : k + 1, :]

    def spread_biases(self):
        r = self.r
        for hq in range(3):
            for w, k in ((0, 4), (2, 5)):
                r.bqkv[hq, :, w * 256 : w * 256 + 256] = r.vec[k : k + 1, hq * 256 : hq * 256 + 256]
            r.bqkv[hq, :, 256:512] = jnp.zeros((1, 256), f32)
        for c in range(CHUNKS):
            for i in range(OWNERS):
                r.bu[c, :, i * 128 : (i + 1) * 128] = r.vec[up_block(c, i)]

    def first_norm(self, g):
        normed, _ = normal(rows_of(self.r.x, g).astype(f32))
        return (normed * self.vec(0) + self.vec(1)).astype(bf)

    def norm_item(self, t):
        r = self.r

        def step(g, _):
            normed, _ = normal(r.x[g, t].astype(f32))
            r.a2[g, t] = (normed * self.vec(0) + self.vec(1)).astype(bf)
            return 0

        lax.fori_loop(0, GROUPS, step, 0)

    def lanes(self, hq, hp, w):
        return pl.ds(pl.multiple_of(hq * D + w * 256 + hp * 128, 128), 128)

    def attend(self, part, hooks):
        r, low = self.r, self.low
        t, hq = part // 3, part % 3
        a1 = r.a2[:, t].reshape(GROUPS * GROUP, D)
        p = nn(a1, r.wqkv[hq].reshape(D, D)) + self.qkv_bias(hq)
        r.qkv[:, t, :, pl.ds(pl.multiple_of(hq * D, 128), D)] = p.astype(bf).reshape(GROUPS, GROUP, D)
        run_hooks(hooks, 3 * part)

        def step(hp, _):
            lanes = [self.lanes(hq, hp, w) for w in range(3)]
            out = pl.ds(pl.multiple_of(hq * 256 + hp * 128, 128), 128)
            k2 = r.qkv[:, t, :, lanes[1]].reshape(GROUPS * GROUP, 128)
            v2 = self.turned(r.qkv[:, t, :, lanes[2]].reshape(GROUPS * GROUP, 128))
            for g in range(GROUPS):
                n = (g + 1) * GROUP
                qs = stacked(r.qkv[g, t, :, lanes[0]] * jnp.asarray(0.125, bf), low)
                s = self.masks(nt(k2[:n], qs), t, g)
                top = jnp.max(s, 0, keepdims=True)
                e = jnp.exp(s - top)
                total = jnp.sum(e, 0, keepdims=True)
                p = (e * (1.0 / total)).astype(bf)
                r.stats[6 * t + 2 * hq + hp, g : g + 1, :] = top + jnp.log(total)
                r.o[g, t, :, out] = self.own_heads(nn(v2[:, :n], p))
            run_hooks(hooks, 3 * part + 1 + hp)
            return 0

        lax.fori_loop(0, 2, step, 0)

    def qkv_bias(self, hq):
        return self.r.bqkv[hq]

    def middle(self, hooks):
        r = self.r

        def step(g, _):
            v = rows_of(r.x, g).astype(f32) + nn(rows_of(r.o, g), r.wo[...].reshape(D, D)) + self.vec(6)
            put_rows(r.x2, g, v)
            put_rows(r.yacc, g, v + self.vec(7))
            normed, _ = normal(v)
            a = (normed * self.vec(2) + self.vec(3)).astype(bf)
            put_rows(r.a2, g, a)
            self.turn_rows(r.a2t, g, a)
            dy = rows_of(r.dy, g)
            self.turn_rows(r.dyt, g, dy)
            put_rows(r.da2, g, jnp.zeros((256, D), f32))
            r.gv[7:8, :] += col_sum(dy.astype(f32))
            run_hooks(hooks, g)
            return 0

        lax.fori_loop(0, GROUPS, step, 0)

    def feed(self, hooks):
        r = self.r

        def column(c, j):
            cols = span256(j)
            wup = r.wup[c, :, :, :, :, cols].reshape(D, 256)
            wdn = r.wdn[c, j].reshape(256, D)
            for k in range(2):
                rows = slice(512 * k, 512 * k + 512)
                u = nn(halves(r.a2, k), wup) + r.bu[c, :, cols]
                u2 = u * u
                half = 0.5 * jnp.tanh(u * (0.7978845608028654 + 0.035677408136300125 * u2)) + 0.5
                r.gl[rows, cols] = (u * half).astype(bf)
                slope = half + u * (2.0 * half * (1.0 - half)) * (
                    0.7978845608028654 + 0.10703222440890037 * u2
                )
                d = (nt(halves(r.dy, k), wdn) * slope).astype(bf)
                r.du[rows, cols] = d
                r.gbu[c, :, cols] += col_sum(d.astype(f32))

        def chunk(c, _):
            def step(j, _):
                column(c, j)
                run_hooks(hooks, 10 * c + j)
                return 0

            def down_grad(h, _):
                down = nn(r.dyt[pl.ds(pl.multiple_of(h * 384, 384), 384), :], r.gl[...]).astype(bf)
                for i in range(OWNERS):
                    r.gdn[c, i // 2, i % 2, h] = down[:, i * 128 : (i + 1) * 128]
                return 0

            def up_back(k, _):
                rows = pl.ds(pl.multiple_of(512 * k, 512), 512)
                back = nt(r.du[rows, :], r.wup[c].reshape(D, WIDE))
                r.da2[pl.ds(2 * k, 2)] += back.reshape(2, 2, GROUP, D)
                return 0

            def up_grad(h, _):
                up = nn(r.a2t[pl.ds(pl.multiple_of(h * 384, 384), 384), :], r.du[...]).astype(bf)
                r.wup[c, pl.ds(2 * h, 2)] = up.reshape(2, 2, 2, 48, WIDE)
                return 0

            def down(k, _):
                rows = pl.ds(pl.multiple_of(512 * k, 512), 512)
                out = nn(r.gl[rows, :], r.wdn[c].reshape(WIDE, D))
                r.yacc[pl.ds(2 * k, 2)] += out.reshape(2, 2, GROUP, D)
                return 0

            lax.fori_loop(0, 4, step, 0)
            for n, act in enumerate((down_grad, up_back, up_grad, down)):
                lax.fori_loop(0, 2, act, 0)
                run_hooks(hooks, 10 * c + 4 + n)
            return 0

        lax.fori_loop(0, CHUNKS, chunk, 0)
        for c in range(CHUNKS):
            for i in range(OWNERS):
                r.gv[up_block(c, i)] = r.gbu[c, :, i * 128 : (i + 1) * 128]

    def turn(self, order, send, hooks):
        r = self.r

        def step(k, _):
            g = order(k)
            c = rows_of(r.da2, g)
            normed, scale = normal(rows_of(r.x2, g))
            r.gv[2:3, :] += col_sum(c * normed)
            r.gv[3:4, :] += col_sum(c)
            d = rows_of(r.dy, g).astype(f32) + norm_back(c, normed, scale, self.vec(2))
            put_rows(r.dy, g, rows_of(r.yacc, g).astype(bf))
            send(k, g)
            put_rows(r.da2, g, d)
            r.gv[6:7, :] += col_sum(d)
            dz = d.astype(bf)
            put_rows(r.a2, g, dz)
            self.turn_rows(r.gl, g, rows_of(r.o, g))
            self.turn_rows(r.du, g, self.first_norm(g))
            put_rows(r.yacc, g, jnp.zeros((256, D), f32))
            run_hooks(hooks, k)
            return 0

        lax.fori_loop(0, GROUPS, step, 0)

    def out_grads(self):
        r = self.r

        def back(k, _):
            rows = pl.ds(2 * k, 2)
            do = nt(r.a2[rows].reshape(512, D), r.wo[...].reshape(D, D)).astype(bf)
            r.o[rows] = do.reshape(2, 2, GROUP, D)
            return 0

        def grad(h, _):
            part = r.gl[pl.ds(pl.multiple_of(h * 384, 384), 384), :]
            grads = nn(part, r.a2[...].reshape(GROUPS * 256, D)).astype(bf)
            r.wo[pl.ds(2 * h, 2)] = grads.reshape(2, 2, 2, 48, D)
            return 0

        lax.fori_loop(0, 2, back, 0)
        lax.fori_loop(0, 2, grad, 0)

    def attend_back(self, hooks, order, send):
        r, low = self.r, self.low

        def pair(hq, t, hp):
            lanes = [self.lanes(hq, hp, w) for w in range(3)]
            out = pl.ds(pl.multiple_of(hq * 256 + hp * 128, 128), 128)
            r.dkv[...] = jnp.zeros_like(r.dkv)
            k2 = r.qkv[:, t, :, lanes[1]].reshape(GROUPS * GROUP, 128)
            v2 = r.qkv[:, t, :, lanes[2]].reshape(GROUPS * GROUP, 128)
            turned_k = self.turned(k2)
            for g in range(GROUPS):
                n = (g + 1) * GROUP
                qs = stacked(r.qkv[g, t, :, lanes[0]] * jnp.asarray(0.125, bf), low)
                dos = stacked(r.o[g, t, :, out], low)
                s = self.masks(nt(k2[:n], qs), t, g)
                p = jnp.exp(s - r.stats[6 * t + 2 * hq + hp, g : g + 1, :])
                dp = nt(v2[:n], dos)
                ds = (p * (dp - jnp.sum(p * dp, 0, keepdims=True))).astype(bf)
                r.dkv[0, :n, :] += nn(ds, qs)
                r.dkv[1, :n, :] += nn(p.astype(bf), dos)
                r.qkv[g, t, :, lanes[0]] = self.own_heads(nn(turned_k[:, :n], ds) * 0.125)
            for w in range(2):
                r.qkv[:, t, :, lanes[w + 1]] = r.dkv[w].astype(bf).reshape(GROUPS, GROUP, 128)

        def quad(hq, _):
            cols = pl.ds(pl.multiple_of(hq * D, 128), D)

            def item(t, _):
                def step(hp, _):
                    pair(hq, t, hp)
                    run_hooks(hooks, 10 * hq + 2 * t + hp)
                    return 0

                lax.fori_loop(0, 2, step, 0)
                pl.when(t == 1)(lambda: grads(hq, cols))
                run_hooks(hooks, 10 * hq + 4 + t)
                rows = r.qkv[:, t, :, cols].reshape(512, D)
                back = nt(rows, r.wqkv[hq].reshape(D, D))
                r.yacc[:, t] += back.reshape(GROUPS, GROUP, D)
                run_hooks(hooks, 10 * hq + 6 + t)

                @pl.when(hq == 2)
                def _():
                    lax.fori_loop(0, GROUPS, lambda k, _: finish(t, k), 0)
                    run_hooks(hooks, 10 * hq + 8 + t)

                return 0

            lax.fori_loop(0, 2, item, 0)
            return 0

        def grads(hq, cols):
            d = r.qkv[:, :, :, cols].reshape(GROUPS * 256, D)

            def grad(h, _):
                part = r.du[pl.ds(pl.multiple_of(h * 384, 384), 384), :]
                out = nn(part, d).astype(bf)
                r.wdn[hq, pl.ds(2 * h, 2), :, :, :48, :] = out.reshape(2, 2, 2, 48, D)
                return 0

            lax.fori_loop(0, 2, grad, 0)
            sums = col_sum(d.astype(f32))
            r.gv[4:5, span256(hq)] = sums[:, :256]
            r.gv[5:6, span256(hq)] = sums[:, 512:]

        def finish(t, k):
            g = order(k)
            c = r.yacc[g, t]
            normed, scale = normal(r.x[g, t].astype(f32))
            r.gv[0:1, :] += col_sum(c * normed)
            r.gv[1:2, :] += col_sum(c)
            d = r.da2[g, t] + norm_back(c, normed, scale, self.vec(0))
            r.x[g, t] = d.astype(bf)
            send(k, t)
            return 0

        lax.fori_loop(0, 3, quad, 0)


class Here:
    def __init__(self):
        self.i, self.b = lax.axis_index("items"), lax.axis_index("blk")
        self.z, self.y = self.i // 2, self.i % 2
        self.x, self.c = self.b // 2, self.b % 2

    def z_plus(self, k):
        return (self.z + k) % 4

    def at_z(self, k):
        return (2 * self.z_plus(k) + self.y, self.b)

    def at_y(self):
        return (self.i + 1 - 2 * self.y, self.b)

    def at_x(self):
        return (self.i, (self.b + 2) % 4)

    def at_core(self):
        return (self.i, self.b + 1 - 2 * self.c)

    def at_blk(self, k):
        return (self.i, (self.b + k) % 4)

    def at_items(self, k):
        return ((self.i + k) % OWNERS, self.b)


def remote(src, dst, send, recv, device):
    return pltpu.make_async_remote_copy(
        src_ref=src, dst_ref=dst, send_sem=send, recv_sem=recv, device_id=device, device_id_type=MESH
    )


class Mail:
    def __init__(self, here, send, recv):
        self.here, self.send, self.recv = here, send, recv

    def go(self, src, dst, slot, device):
        remote(src, dst, self.send.at[slot], self.recv.at[slot], device).start()

    def arrived(self, dst, slot):
        remote(dst, dst, self.send.at[slot], self.recv.at[slot], self.here.at_core()).wait_recv()

    def left(self, src, *slots):
        for slot in slots:
            remote(src, src, self.send.at[slot], self.recv.at[slot], self.here.at_core()).wait_send()


class Gather(Mail):
    slots = 5

    def __init__(self, here, dst, send, recv):
        super().__init__(here, send, recv)
        self.dst = dst

    def first(self):
        h = self.here
        own = self.dst.at[h.z, h.y, h.c]
        for k in (1, 2, 3):
            self.go(own, own, k - 1, h.at_z(k))

    def second(self):
        h = self.here
        for k in (1, 2, 3):
            self.arrived(self.dst.at[h.z_plus(4 - k), h.y, h.c], k - 1)
        line = self.dst.at[:, h.y, h.c]
        self.go(line, line, 3, h.at_y())

    def third(self):
        h = self.here
        self.arrived(self.dst.at[:, 1 - h.y, h.c], 3)
        half = self.dst.at[:, :, h.c]
        self.go(half, half, 4, h.at_core())

    def last(self):
        self.arrived(self.dst.at[:, :, 1 - self.here.c], 4)

    def drain(self):
        self.left(self.dst.at[0, 0, 0], 0, 1, 2)
        self.left(self.dst.at[:, 0, 0], 3)
        self.left(self.dst.at[:, :, 0], 4)


class SplitGather(Gather):
    slots = 6

    def mine(self, z, y):
        h = self.here
        return self.dst.at[z, y, h.c, :, self.columns(h.x)]

    def columns(self, x):
        width = self.dst.shape[-1] // 2
        return pl.ds(pl.multiple_of(x * width, width), width)

    def first(self):
        h = self.here
        own = self.mine(h.z, h.y)
        for k in (1, 2, 3):
            self.go(own, own, k - 1, h.at_z(k))

    def second(self):
        h = self.here
        for k in (1, 2, 3):
            self.arrived(self.mine(h.z_plus(4 - k), h.y), k - 1)
        line = self.mine(slice(None), h.y)
        self.go(line, line, 3, h.at_y())

    def across(self):
        h = self.here
        self.arrived(self.mine(slice(None), 1 - h.y), 3)
        part = self.mine(slice(None), slice(None))
        self.go(part, part, 5, h.at_x())

    def third(self):
        h = self.here
        self.arrived(self.dst.at[:, :, h.c, :, self.columns(1 - h.x)], 5)
        half = self.dst.at[:, :, h.c]
        self.go(half, half, 4, h.at_core())

    def drain(self):
        self.left(self.mine(0, 0), 0, 1, 2)
        self.left(self.mine(slice(None), 0), 3)
        self.left(self.dst.at[:, :, 0], 4)
        self.left(self.mine(slice(None), slice(None)), 5)


class Exchange(Mail):
    def __init__(self, here, src, dst, send, recv, local):
        super().__init__(here, send, recv)
        self.src, self.dst, self.local = src, dst, local

    def own(self):
        h = self.here
        return pltpu.make_async_copy(self.src.at[h.b], self.dst.at[h.b], self.local)

    def order(self, k):
        h = self.here
        odd, near = k % 2, k // 2
        far = (1 - odd) * ((h.b + 2) % 4) + odd * (3 - h.b)
        return (1 - near) * far + near * (h.b + (1 - odd) * (1 - 2 * h.c))

    def copy(self, k):
        h = self.here
        to = self.order(k)
        return remote(self.src.at[to], self.dst.at[h.b], self.send.at[k], self.recv.at[k], (h.i, to))

    def put(self, k, _=None):
        @pl.when(k < 3)
        def _():
            self.copy(k).start()

        @pl.when(k == 3)
        def _():
            self.own().start()

    def start(self):
        for k in range(3):
            self.copy(k).start()
        self.own().start()

    def arrive(self):
        self.own().wait()
        for k in range(3):
            self.arrived(self.dst.at[self.order(k)], k)

    def drain(self):
        for k in range(3):
            self.copy(k).wait_send()


class ItemExchange(Exchange):
    def copy(self, k, t):
        h = self.here
        to, slot = self.order(k), 3 * t + k
        return remote(
            self.src.at[to, t], self.dst.at[h.b, t], self.send.at[slot], self.recv.at[slot], (h.i, to)
        )

    def own(self, t):
        h = self.here
        return pltpu.make_async_copy(self.src.at[h.b, t], self.dst.at[h.b, t], self.local.at[t])

    def put(self, k, t):
        @pl.when(k < 3)
        def _():
            self.copy(k, t).start()

        @pl.when(k == 3)
        def _():
            self.own(t).start()

    def start(self):
        for t in range(2):
            for k in range(3):
                self.copy(k, t).start()
            self.own(t).start()

    def arrive(self, t):
        self.own(t).wait()
        for k in range(3):
            self.arrived(self.dst.at[self.order(k), t], 3 * t + k)

    def drain(self):
        self.left(self.src.at[0, 0], *range(6))


class Reduce(Mail):
    slots = 8

    def __init__(self, here, g, rc, place, count, credit, ry, rz, rx, total, out, send, recv):
        super().__init__(here, send, recv)
        self.g, self.rc, self.place, self.count, self.credit = g, rc, place, count, credit
        self.ry, self.rz, self.rx, self.total, self.out = ry, rz, rx, total, out

    def over_core(self):
        h = self.here
        if self.place is not None and self.place >= 2:
            pl.semaphore_wait(self.credit, 1)
        self.go(self.g.at[:, :, 1 - h.c], self.rc, 0, h.at_core())

    def over_y(self):
        h = self.here
        self.arrived(self.rc, 0)

        def add(n, _):
            z, y = n // 2, n % 2
            self.g[z, y, h.c] = self.g[z, y, h.c] + self.rc[z, y]
            return 0

        lax.fori_loop(0, 8, add, 0)
        if self.place is not None and self.place + 2 < self.count:
            pl.semaphore_signal(self.credit, inc=1, device_id=h.at_core(), device_id_type=MESH)
        self.go(self.g.at[:, 1 - h.y, h.c], self.ry, 1, h.at_y())

    def over_z(self):
        h = self.here
        self.arrived(self.ry, 1)

        def add(z, _):
            self.g[z, h.y, h.c] = self.g[z, h.y, h.c] + self.ry[z]
            return 0

        lax.fori_loop(0, 4, add, 0)
        for k in (2, 1, 3):
            self.go(self.g.at[h.z_plus(k), h.y, h.c], self.rz.at[k - 1], 1 + k, h.at_z(k))

    def over_x(self):
        h = self.here
        part = self.g[h.z, h.y, h.c].astype(f32)
        for k in (1, 2, 3):
            self.arrived(self.rz.at[k - 1], 1 + k)
            part = part + self.rz[k - 1].astype(f32)
        self.total[0] = part.astype(bf)
        self.go(self.total.at[0], self.rx, 5, h.at_x())

    def share(self):
        h = self.here
        self.arrived(self.rx, 5)
        self.total[1] = self.total[0] + self.rx[...]
        self.own().start()
        self.go(self.total.at[1], self.out.at[h.c], 6, h.at_core())

    def own(self):
        return pltpu.make_async_copy(self.total.at[1], self.out.at[self.here.c], self.send.at[7])

    def last(self):
        self.arrived(self.out.at[1 - self.here.c], 6)
        self.own().wait()

    def drain(self):
        self.left(self.rc, 0)
        self.left(self.ry, 1)
        self.left(self.rz.at[0], 2, 3, 4)
        self.left(self.rx, 5, 6)


class SplitReduce(Reduce):
    slots = 9

    def __init__(self, rx0, *args):
        super().__init__(*args)
        self.rx0 = rx0

    def rows(self, x):
        count = self.g.shape[-2] // 2
        return pl.ds(pl.multiple_of(x * count, count), count)

    def over_x0(self):
        h = self.here
        self.arrived(self.rc, 0)

        def add(n, _):
            z, y = n // 2, n % 2
            self.g[z, y, h.c] = self.g[z, y, h.c] + self.rc[z, y]
            return 0

        lax.fori_loop(0, 8, add, 0)
        if self.place + 2 < self.count:
            pl.semaphore_signal(self.credit, inc=1, device_id=h.at_core(), device_id_type=MESH)
        self.go(self.g.at[:, :, h.c, self.rows(1 - h.x)], self.rx0, 8, h.at_x())

    def over_y(self):
        h = self.here
        mine = self.rows(h.x)
        self.arrived(self.rx0, 8)

        def add(n, _):
            z, y = n // 2, n % 2
            self.g[z, y, h.c, mine] = self.g[z, y, h.c, mine] + self.rx0[z, y]
            return 0

        lax.fori_loop(0, 8, add, 0)
        self.go(self.g.at[:, 1 - h.y, h.c, mine], self.ry.at[:, self.rows(0)], 1, h.at_y())

    def over_z(self):
        h = self.here
        mine, box = self.rows(h.x), self.rows(0)
        self.arrived(self.ry.at[:, box], 1)

        def add(z, _):
            self.g[z, h.y, h.c, mine] = self.g[z, h.y, h.c, mine] + self.ry[z, box]
            return 0

        lax.fori_loop(0, 4, add, 0)
        for k in (2, 1, 3):
            self.go(self.g.at[h.z_plus(k), h.y, h.c, mine], self.rz.at[k - 1, box], 1 + k, h.at_z(k))

    def over_x(self):
        h = self.here
        mine, box = self.rows(h.x), self.rows(0)
        part = self.g[h.z, h.y, h.c, mine].astype(f32)
        for k in (1, 2, 3):
            self.arrived(self.rz.at[k - 1, box], 1 + k)
            part = part + self.rz[k - 1, box].astype(f32)
        self.total[1, mine] = part.astype(bf)
        done = self.total.at[1, mine]
        self.go(done, done, 5, h.at_x())

    def share(self):
        h = self.here
        self.arrived(self.total.at[1, self.rows(1 - h.x)], 5)
        self.own().start()
        self.go(self.total.at[1], self.out.at[h.c], 6, h.at_core())

    def drain(self):
        box = self.rows(0)
        self.left(self.rc, 0)
        self.left(self.ry.at[:, box], 1)
        self.left(self.rz.at[0, box], 2, 3, 4)
        self.left(self.total.at[1, box], 5)
        self.left(self.rx, 6)
        self.left(self.rx0, 8)


WINDOW = 256


def window_start(owner):
    return (3 * owner // 4 - owner // 7) * 128


def window_of(owner):
    return pl.ds(pl.multiple_of(window_start(owner), 128), WINDOW)


class ReduceVectors(Mail):
    def __init__(self, here, v, blk_inbox, items_inbox, out, send, recv):
        super().__init__(here, send, recv)
        self.v, self.blk_inbox, self.items_inbox, self.out = v, blk_inbox, items_inbox, out

    def first(self):
        h = self.here
        self.blk_inbox[h.b] = self.v[...]
        for k in (1, 2, 3):
            self.go(self.v, self.blk_inbox.at[h.b], k - 1, h.at_blk(k))

    def second(self):
        h = self.here
        for k in (1, 2, 3):
            self.arrived(self.blk_inbox.at[(h.b + 4 - k) % 4], k - 1)
        self.left(self.v, 0, 1, 2)
        box = self.blk_inbox
        self.v[...] = (box[0] + box[1]) + (box[2] + box[3])
        for k in range(1, OWNERS):
            owner = (h.i + k) % OWNERS
            self.go(
                self.v.at[:, window_of(owner)], self.items_inbox.at[h.i], 2 + k, h.at_items(k)
            )
        self.items_inbox[h.i] = self.v[:, window_of(h.i)]

    def third(self):
        h = self.here
        for k in range(1, OWNERS):
            self.arrived(self.items_inbox.at[(h.i + OWNERS - k) % OWNERS], 2 + k)
        total = self.items_inbox[0]
        for n in range(1, OWNERS):
            total = total + self.items_inbox[n]
        self.out[...] = total

    def drain(self):
        self.left(self.out, *range(3, 10))


INBOXES = (("d", CHUNKS, 384, 128), ("u", CHUNKS, 48, WIDE), ("q", 4, 48, D))
COMM_BUFFERS = dict(
    rcd=((2, 4, 2, 384, 128), bf),
    rcu=((2, 4, 2, 48, WIDE), bf),
    vbox=((OWNERS, VROWS, WINDOW), bf),
    gbox=((GROUPS, VROWS, D), f32),
    wbox=((OWNERS, VROWS, WINDOW), f32),
    gvw=((VROWS, WINDOW), f32),
    rx0=((2, 4, 2, 192, 128), bf),
)
for _kind, _n, _rows, _cols in INBOXES:
    COMM_BUFFERS["ry" + _kind] = ((_n, 4, _rows, _cols), bf)
    COMM_BUFFERS["rz" + _kind] = ((_n, 3, _rows, _cols), bf)
    COMM_BUFFERS["rx" + _kind] = ((_n, _rows, _cols), bf)
    COMM_BUFFERS["tt" + _kind] = ((_n, 2, _rows, _cols), bf)
SEMS = dict(
    load=(11,),
    gsend=(13, SplitGather.slots),
    grecv=(13, SplitGather.slots),
    rsend=(12, SplitReduce.slots),
    rrecv=(12, SplitReduce.slots),
    xsend=(2, 6),
    xrecv=(2, 6),
    xlocal=(2, 2),
    esend=(2, 3),
    erecv=(2, 3),
    local=(5,),
    vsend=(7,),
    vrecv=(7,),
    wsend=(10,),
    wrecv=(10,),
)


SPLIT_UP = (0, 1, 2)
SPLIT_DOWN = (1, 2)
MOVES = dict(
    a="first", l="second", xx="across", h="third", w="last",
    core="over_core", x0="over_x0", y="over_y", z="over_z", x="over_x", sh="share", end="last",
)
TIMETABLE = dict(
    start=(("Q0q", "a"), ("Q0k", "a"), ("Q0v", "a"),),
    table=(("Q0q", "l"), ("Q0k", "l"), ("Q1", "a"), ("Q0q", "h"), ("Q0v", "l"), ("Q2", "a"), ("Q0k", "h"), ("Q0q", "w"),),
    ln0=(("Q0v", "h"), ("Q0k", "w"), ("Q0v", "w"),),
    s0a=(("Q1", "l"), ("O", "a"),),
    s0b=(("Q2", "l"), ("U0", "a"), ("Q1", "h"), ("Q1", "w"),),
    s1p=(("O", "l"), ("D0", "a"),),
    s1b=(("Q2", "h"), ("U0", "l"), ("U1", "a"), ("Q2", "w"),),
    s2a=(("O", "h"),),
    s3a=(("O", "w"), ("U0", "xx"), ("D0", "l"), ("D1", "a"),),
    s4b=(("U1", "l"), ("U2", "a"),),
    m1=(("U0", "h"), ("D0", "h"),),
    m3=(("D1", "l"), ("D2", "a"), ("U0", "w"), ("U1", "xx"), ("D0", "w"),),
    f00=(("U2", "l"),),
    f03=(("D1", "h"),),
    g00=(("U1", "h"), ("d0", "core"),),
    g01=(("D1", "w"), ("U2", "xx"), ("D2", "l"),),
    g02=(("U1", "w"), ("u0", "core"),),
    f10=(("d0", "y"),),
    f11=(("u0", "y"),),
    f13=(("U2", "h"), ("D2", "h"),),
    g10=(("d1", "core"),),
    g11=(("U2", "w"),),
    g12=(("u1", "core"),),
    g13=(("D2", "w"), ("d0", "z"),),
    f20=(("d1", "x0"),),
    f21=(("u1", "y"),),
    g20=(("u0", "z"), ("d2", "core"),),
    g21=(("d0", "x"),),
    g22=(("d1", "y"), ("d2", "x0"), ("u2", "core"),),
    g23=(("d0", "sh"),),
    t1=(("u1", "z"), ("u2", "y"), ("d0", "end"),),
    t3=(("u0", "x"),),
    gwo=(("d1", "z"), ("o", "core"),),
    b00=(("d2", "y"),),
    b01=(("o", "y"),),
    b02=(("u1", "x"),),
    b03=(("u2", "z"),),
    gq0=(("d1", "x"), ("q0", "core"),),
    b10=(("d2", "z"),),
    b11=(("q0", "y"),),
    b13=(("o", "z"), ("u2", "x"),),
    gq1=(("q1", "core"),),
    on11=(("u0", "sh"),),
    b20=(("u1", "sh"), ("d2", "x"),),
    b21=(("u0", "end"), ("d1", "sh"), ("u1", "end"), ("q0", "z"), ("q1", "y"),),
    on20=(("u2", "sh"), ("d1", "end"),),
    fin0=(("d2", "sh"),),
    b22=(("u2", "end"), ("o", "x"), ("d2", "end"),),
    gq2=(("q2q", "core"), ("q2k", "core"), ("q2v", "core"),),
    on21=(("q1", "z"),),
    fin1=(("q2q", "y"), ("q2k", "y"), ("q0", "x"),),
    tail0=(("q2v", "y"), ("o", "sh"), ("q2q", "z"), ("o", "end"), ("q2k", "z"), ("q1", "x"), ("q2v", "z"), ("q2q", "x"), ("q2k", "x"), ("q0", "sh"), ("q2v", "x"),),
    tail1=(("q0", "end"), ("q1", "sh"), ("q2q", "sh"), ("q2k", "sh"), ("q2v", "sh"), ("q1", "end"), ("q2q", "end"),),
    tail2=(("q2k", "end"), ("q2v", "end"),),
)


def step_kernel(*refs):
    (xs, dys, counts, masks, w_qkv, w_o, w_up, w_dn, w_vec, y, dx, gv, o_dn, o_up, o_o, o_q) = refs[:16]
    names = list(LAYER_BUFFERS) + list(COMM_BUFFERS) + list(SEMS) + ["credit_d", "credit_u"]
    r = collections.namedtuple("Refs", names)(*refs[16:])
    here = Here()
    barrier = pltpu.get_barrier_semaphore()
    friends = [here.at_items(k) for k in range(1, OWNERS)] + [here.at_blk(k) for k in (1, 2, 3)]
    for device in friends:
        pl.semaphore_signal(barrier, inc=1, device_id=device, device_id_type=MESH)

    half = pl.ds(here.c * 48, 48)
    small, small_dn = pl.ds(0, 48), pl.ds(0, 64)
    loads = []
    for q in range(3):
        loads.append((w_qkv.at[half, pl.ds(q * D, D)], r.x2.at[q // 2, q % 2, small, :]))
    loads.append((w_o.at[half], r.x2.at[1, 1, small, :]))
    for q in range(4):
        loads.append((w_up.at[half, pl.ds(q * D, D)], r.x2.at[2 + q // 2, q % 2, small, :]))
    for q in range(3):
        rows = pl.ds(q * 128 + here.c * 64, 64)
        loads.append((w_dn.at[rows], r.yacc.at[q // 2, q % 2, small_dn, :]))
    loads = [pltpu.make_async_copy(s, d, r.load.at[n]) for n, (s, d) in enumerate(loads)]
    for load in loads:
        load.start()

    layer = Layer(r, Masks(counts, masks))
    for q in range(3):
        loads[q].wait()
        part = r.x2[q // 2, q % 2, :48, :].astype(bf)
        for hq in range(3):
            r.wqkv[hq, here.z, here.y, here.c, :, q * 256 : q * 256 + 256] = part[:, hq * 256 : hq * 256 + 256]
    pl.semaphore_wait(barrier, len(friends))

    x_in = ItemExchange(here, xs, r.x, r.xsend.at[0], r.xrecv.at[0], r.xlocal.at[0])
    dy_in = Exchange(here, dys, r.dy, r.esend.at[0], r.erecv.at[0], r.local.at[1])
    y_out = Exchange(here, r.dy, y, r.esend.at[1], r.erecv.at[1], r.local.at[2])
    dx_out = ItemExchange(here, r.x, dx, r.xsend.at[1], r.xrecv.at[1], r.xlocal.at[1])

    def gather(dst, n):
        return Gather(here, dst, r.gsend.at[n], r.grecv.at[n])

    g_q = [gather(r.wqkv.at[0, :, :, :, :, pl.ds(256 * w, 256)], 10 + w) for w in range(3)]
    g_q += [gather(r.wqkv.at[hq], hq) for hq in (1, 2)]
    g_o = gather(r.wo, 3)
    g_u = [
        (SplitGather if c in SPLIT_UP else Gather)(here, r.wup.at[c], r.gsend.at[4 + c], r.grecv.at[4 + c])
        for c in range(CHUNKS)
    ]
    g_d = [gather(r.wdn.at[c], 7 + c) for c in range(CHUNKS)]

    def reduce(kind, n, index, g, rc, place, count, credit, out):
        boxes = [getattr(r, box + kind).at[n] for box in ("ry", "rz", "rx", "tt")]
        args = (here, g, rc, place, count, credit, *boxes, out, r.rsend.at[index], r.rrecv.at[index])
        if kind == "d" and n in SPLIT_DOWN:
            return SplitReduce(r.rx0.at[n - 1], *args)
        return Reduce(*args)

    s_d = [
        reduce("d", c, 2 * c, r.gdn.at[c], r.rcd.at[c % 2], c, 3, r.credit_d, o_dn.at[c])
        for c in range(CHUNKS)
    ]
    s_u = [
        reduce("u", c, 2 * c + 1, r.wup.at[c], r.rcu.at[c % 2], c, 7, r.credit_u, o_up.at[c])
        for c in range(CHUNKS)
    ]
    narrow = [r.rcu.at[n % 2, :, :, :, pl.ds(0, D)] for n in range(2)]
    s_o = reduce("q", 3, 6, r.wo, narrow[1], 3, 7, r.credit_u, o_o)
    s_q = [
        reduce("q", c, 7 + c, layer.qkv_grad(c), narrow[c % 2], 4 + c, 7, r.credit_u, o_q.at[c])
        for c in range(2)
    ]
    for w in range(3):
        third = pl.ds(256 * w, 256)
        boxes = [r.ryq.at[2, :, :, third], r.rzq.at[2, :, :, third], r.rxq.at[2, :, third], r.ttq.at[2, :, :, third]]
        s_q.append(
            Reduce(
                here, r.wdn.at[2, :, :, :, pl.ds(0, 48), third], r.rcu.at[0, :, :, :, third],
                6 if w == 0 else None, 7, r.credit_u, *boxes, o_q.at[2, :, :, third],
                r.rsend.at[9 + w], r.rrecv.at[9 + w],
            )
        )
    sums = ReduceVectors(here, r.gv, r.gbox, r.wbox, r.gvw, r.wsend, r.wrecv)

    units = {"O": g_o, "o": s_o}
    for c in range(CHUNKS):
        units |= {f"U{c}": g_u[c], f"D{c}": g_d[c], f"d{c}": s_d[c], f"u{c}": s_u[c]}
    units |= dict(zip(("Q0q", "Q0k", "Q0v", "Q1", "Q2"), g_q))
    units |= dict(zip(("q0", "q1", "q2q", "q2k", "q2v"), s_q))

    def at(slot):
        for unit, name in TIMETABLE.get(slot, ()):
            getattr(units[unit], MOVES[name])()

    def slots(**names):
        return {
            index: (lambda slot=slot: at(slot)) for slot, index in names.items() if slot in TIMETABLE
        }

    at("start")
    x_in.start()
    at("more")

    rows = lax.broadcasted_iota(jnp.int32, (96, WINDOW), 0)
    cols = lax.broadcasted_iota(jnp.int32, (96, WINDOW), 1)
    chosen = jnp.where(cols - (here.i * 96 - window_start(here.i)) == rows, 1.0, 0.0).astype(bf)
    r.vbox[here.i] = jnp.concatenate(
        [nn(w_vec[...].astype(bf), chosen), jnp.zeros((VROWS - 12, WINDOW), f32)], 0
    ).astype(bf)
    table = Mail(here, r.vsend, r.vrecv)
    for k in range(1, OWNERS):
        own = r.vbox.at[here.i]
        table.go(own, own, k - 1, here.at_items(k))
    layer.start()
    loads[3].wait()
    r.wo[here.z, here.y, here.c] = r.x2[1, 1, :48, :].astype(bf)
    for q in range(4):
        loads[4 + q].wait()
        part = r.x2[2 + q // 2, q % 2, :48, :].astype(bf)
        for m in range(6):
            i, c = (6 * q + m) // 3, (6 * q + m) % 3

            def put(i=i, c=c, part=part[:, m * 128 : (m + 1) * 128]):
                r.wup[c, here.z, here.y, here.c, :, i * 128 : (i + 1) * 128] = part

            if c in SPLIT_UP:
                pl.when(here.x == i // 4)(put)
            else:
                put()
    for c in range(CHUNKS):
        loads[8 + c].wait()
        r.wdn[c, here.z, here.y, here.c] = r.yacc[c // 2, c % 2, :64, :].astype(bf)

    at("cast")
    for k in range(1, OWNERS):
        table.arrived(r.vbox.at[(here.i + OWNERS - k) % OWNERS], k - 1)
    r.vec[...] = jnp.zeros_like(r.vec)
    for n in range(OWNERS):
        start = window_start(n)
        r.vec[:, start : start + WINDOW] += r.vbox[n].astype(f32)
    layer.spread_biases()
    at("table")
    x_in.arrive(0)
    layer.norm_item(0)
    at("ln0")

    def other_item():
        x_in.arrive(1)
        layer.norm_item(1)

    in_parts = slots(**{f"s{n}{'pab'[j]}": 3 * n + j for n in range(6) for j in range(3)})
    for index, extra in ((2, dy_in.start), (8, other_item)):

        def both(before=in_parts.get(index, lambda: None), extra=extra):
            before()
            extra()

        in_parts[index] = both

    def part(n, _):
        layer.attend(n, in_parts)
        return 0

    lax.fori_loop(0, 6, part, 0)
    dy_in.arrive()
    at("dy")
    layer.middle(slots(**{f"m{k}": k for k in range(GROUPS)}))
    in_feed = {f"f{c}{j}": 10 * c + j for c in range(CHUNKS) for j in range(4)}
    in_feed |= {f"g{c}{n}": 10 * c + 4 + n for c in range(CHUNKS) for n in range(4)}
    in_feed = slots(**in_feed)
    for c in range(CHUNKS):

        def overwrite(c=c, before=in_feed.get(10 * c + 5, lambda: None)):
            before()
            g_u[c].drain()

        in_feed[10 * c + 5] = overwrite
    layer.feed(in_feed)
    dy_in.drain()
    layer.turn(y_out.order, y_out.put, slots(**{f"t{k}": k for k in range(GROUPS)}))
    g_o.drain()
    for c in range(CHUNKS):
        g_d[c].drain()
    layer.out_grads()
    at("gwo")
    in_back = {f"b{q}{k}": 10 * q + k for q in range(3) for k in range(4)}
    in_back |= {f"gq{q}": 10 * q + 5 for q in range(3)}
    in_back |= {f"on{q}{t}": 10 * q + 6 + t for q in range(3) for t in range(2)}
    in_back |= {f"fin{t}": 28 + t for t in range(2)}
    layer.attend_back(slots(**in_back), dx_out.order, dx_out.put)
    sums.first()
    y_out.arrive()
    for part in g_q + [x_in, y_out]:
        part.drain()
    table.left(r.vbox.at[0], *range(OWNERS - 1))
    at("tail0")
    sums.second()
    for part in s_d + s_u + [s_o]:
        part.drain()
    at("tail1")
    sums.third()
    store = pltpu.make_async_copy(r.gvw, gv, r.local.at[4])
    store.start()
    at("tail2")
    dx_out.arrive(0)
    dx_out.arrive(1)
    store.wait()
    for part in s_q + [sums, dx_out]:
        part.drain()


def step(x, dy, counts, masks, weights):
    scratch = [pltpu.VMEM(*spec) for spec in (LAYER_BUFFERS | COMM_BUFFERS).values()]
    scratch += [pltpu.SemaphoreType.DMA(shape) for shape in SEMS.values()]
    scratch += [pltpu.SemaphoreType.REGULAR] * 2
    return pl.pallas_call(
        step_kernel,
        out_shape=(
            jax.ShapeDtypeStruct(TOKENS, bf),
            jax.ShapeDtypeStruct(TOKENS, bf),
            jax.ShapeDtypeStruct((VROWS, WINDOW), f32),
            jax.ShapeDtypeStruct((CHUNKS, 2, 384, 128), bf),
            jax.ShapeDtypeStruct((CHUNKS, 2, 48, WIDE), bf),
            jax.ShapeDtypeStruct((2, 48, D), bf),
            jax.ShapeDtypeStruct((3, 2, 48, D), bf),
        ),
        in_specs=[ANY, ANY, SMEM, SMEM, ANY, ANY, ANY, ANY, VMEM],
        out_specs=[ANY] * 7,
        scratch_shapes=scratch,
        compiler_params=pltpu.CompilerParams(
            collective_id=1, has_side_effects=True, vmem_limit_bytes=63 * MIB + 512 * 1024
        ),
    )(x, dy, counts, masks, *weights)


def update_kernel(*refs):
    states = [refs[5 * n : 5 * n + 5] for n in range(3)]
    gv, *grads_in, y_in, dx_in = refs[15:22]
    y, dx = refs[22:24]
    news = [refs[24 + 5 * n : 29 + 5 * n] for n in range(3)]
    b_qkv, b_o, b_up, b_dn, g_dn, g_up, g_o, g_q, out, low, wide, s_in, s_out, s_grad, s_tok = refs[39:]
    boxes = (b_qkv, b_o, b_up, b_dn)
    load_y = pltpu.make_async_copy(y_in, out, s_tok.at[0])
    load_dx = pltpu.make_async_copy(dx_in, low, s_tok.at[1])
    store_dx = pltpu.make_async_copy(wide, dx, s_tok.at[2])
    store_y = pltpu.make_async_copy(out, y, s_tok.at[3])
    grad_loads = [
        pltpu.make_async_copy(src, dst, s_grad.at[n])
        for n, (src, dst) in enumerate(zip(grads_in, (g_dn, g_up, g_o, g_q)))
    ]
    parts = [(1, pl.ds(0, 96))]
    parts += [(2, pl.ds(48 * h, 48)) for h in range(2)]
    parts += [(0, pl.ds(48 * h, 48)) for h in range(2)]
    parts += [(3, pl.ds(128 * c, 128)) for c in range(CHUNKS)]

    def load(n):
        a, rows = parts[n]
        return [
            pltpu.make_async_copy(states[k][a].at[rows], boxes[a].at[k, rows], s_in.at[n, k]) for k in range(3)
        ]

    def store(n):
        a, rows = parts[n]
        return [
            pltpu.make_async_copy(boxes[a].at[k, rows], news[k][a].at[rows], s_out.at[n, k]) for k in range(3)
        ]

    def start(copies):
        for copy in copies:
            copy.start()

    def wait(copies):
        for copy in copies:
            copy.wait()

    start([grad_loads[2]] + load(0) + [grad_loads[1]] + load(1) + load(2))
    start([grad_loads[3], load_dx, load_y])

    def update(a, rows, cols, grad):
        box = boxes[a]
        new = adamw(
            box[0, rows, cols], box[1, rows, cols], box[2, rows, cols], grad.astype(f32), rates[a], decays[a]
        )
        for k in range(3):
            box[k, rows, cols] = new[k]

    for n, (a, rows) in enumerate(parts):
        if n + 3 < len(parts):
            if n + 3 == 5:
                start([grad_loads[0]])
            start(load(n + 3))
        if n in (0, 1, 3, 5):
            grad_loads[(2, 1, None, 3, None, 0)[n]].wait()
        wait(load(n))
        if a == 1:
            for h in range(2):
                update(1, slice(48 * h, 48 * h + 48), slice(0, D), g_o[h])
        elif a == 2:
            h = n - 1
            for c in range(CHUNKS):
                for i in range(OWNERS):
                    cols = slice((3 * i + c) * 128, (3 * i + c + 1) * 128)
                    update(2, slice(48 * h, 48 * h + 48), cols, g_up[c, h, :, i * 128 : (i + 1) * 128])
        elif a == 0:
            h = n - 3
            for hq in range(3):
                for w in range(3):
                    cols = slice(w * D + hq * 256, w * D + hq * 256 + 256)
                    update(0, slice(48 * h, 48 * h + 48), cols, g_q[hq, h, :, w * 256 : w * 256 + 256])
        else:
            c = n - 5
            for h in range(2):
                update(
                    3,
                    slice(128 * c, 128 * c + 128),
                    slice(384 * h, 384 * h + 384),
                    g_dn[c, h].astype(f32).T,
                )
        start(store(n))
        if n == 2:
            load_dx.wait()
            wide[...] = low[...].astype(f32)
            load_y.wait()
            start([store_dx, store_y])

    here = lax.axis_index("items")
    first = here * 96 - window_start(here)
    rows = lax.broadcasted_iota(jnp.int32, (WINDOW, 96), 0)
    cols = lax.broadcasted_iota(jnp.int32, (WINDOW, 96), 1)
    chosen = jnp.where(rows - first == cols, 1.0, 0.0)
    grad = jnp.dot(gv[...], chosen, preferred_element_type=f32, precision=lax.Precision.HIGHEST)
    new = adamw(states[0][4][...], states[1][4][...], states[2][4][...], grad[:12], rates[4], decays[4])
    for k in range(3):
        news[k][4][...] = new[k]
    for n in range(len(parts)):
        wait(store(n))
    wait([store_dx, store_y])


def update(masters, firsts, seconds, gv, grads, y, dx):
    big = [ANY] * 4 + [VMEM]
    shapes = [jax.ShapeDtypeStruct(m.shape, f32) for m in masters]
    out = pl.pallas_call(
        update_kernel,
        out_shape=[jax.ShapeDtypeStruct(TOKENS, bf), jax.ShapeDtypeStruct(TOKENS, f32)] + shapes * 3,
        in_specs=big * 3 + [VMEM] + [ANY] * 6,
        out_specs=[ANY, ANY] + big * 3,
        scratch_shapes=[
            pltpu.VMEM((3, 96, 3 * D), f32),
            pltpu.VMEM((3, 96, D), f32),
            pltpu.VMEM((3, 96, FF), f32),
            pltpu.VMEM((3, 384, D), f32),
        ]
        + [pltpu.VMEM(g.shape, bf) for g in grads]
        + [
            pltpu.VMEM(TOKENS, bf),
            pltpu.VMEM(TOKENS, bf),
            pltpu.VMEM(TOKENS, f32),
            pltpu.SemaphoreType.DMA((8, 3)),
            pltpu.SemaphoreType.DMA((8, 3)),
            pltpu.SemaphoreType.DMA((4,)),
            pltpu.SemaphoreType.DMA((4,)),
        ],
        compiler_params=pltpu.CompilerParams(vmem_limit_bytes=63 * MIB),
    )(*masters, *firsts, *seconds, gv, *grads, y, dx)
    return out[0], out[1], [out[2 + 5 * k : 7 + 5 * k] for k in range(3)]


def plain_kernel(*refs):
    (xs, dys, counts, masks, w_qkv, w_o, w_up, w_dn, vecs, y, dx, gv, o_dn, o_up, o_o, o_q) = refs[:16]
    r = collections.namedtuple("Refs", list(LAYER_BUFFERS) + ["sem"])(*refs[16:])
    layer = Layer(r, Masks(counts, masks))
    loads = [(xs, r.x), (dys, r.dy), (w_qkv, r.wqkv), (w_o, r.wo), (w_up, r.wup), (w_dn, r.wdn), (vecs, r.vec)]

    def move(pairs):
        copies = [pltpu.make_async_copy(s, d, r.sem.at[n]) for n, (s, d) in enumerate(pairs)]
        for copy in copies:
            copy.start()
        for copy in copies:
            copy.wait()

    move(loads)
    layer.start()
    layer.spread_biases()
    for t in range(2):
        layer.norm_item(t)

    def part(n, _):
        layer.attend(n, {})
        return 0

    lax.fori_loop(0, 6, part, 0)
    layer.middle({})
    layer.feed({})
    move([(r.wup, o_up), (r.gdn, o_dn)])
    layer.turn(lambda k: k, lambda k, g: None, {})
    layer.out_grads()
    layer.attend_back({}, lambda k: k, lambda k, t: None)
    move(
        [(r.dy, y), (r.x, dx), (r.gv, gv), (r.wo, o_o)]
        + [(layer.qkv_grad(hq), o_q.at[hq]) for hq in range(3)]
    )


def plain_step(x, dy, counts, masks, weights):
    def swap(values):
        return lax.all_to_all(values, "blk", 0, 0, tiled=True)

    full = [lax.all_gather(w.astype(bf), "items", axis=0, tiled=True) for w in weights[:4]]
    vecs = lax.all_gather(weights[4].astype(bf), "items", axis=1, tiled=True).astype(f32)
    w_qkv = full[0].reshape(D, 3, 3, 256).transpose(2, 0, 1, 3).reshape(3, 4, 2, 2, 48, D)
    w_o = full[1].reshape(4, 2, 2, 48, D)
    w_up = full[2].reshape(D, OWNERS, CHUNKS, 128).transpose(2, 0, 1, 3).reshape(CHUNKS, 4, 2, 2, 48, WIDE)
    w_dn = full[3].reshape(OWNERS, CHUNKS, 128, D).transpose(1, 0, 2, 3).reshape(CHUNKS, 4, 2, 2, 64, D)
    vecs = jnp.pad(vecs, ((0, VROWS - vecs.shape[0]), (0, 0)))
    y, dx, gv, g_dn, g_up, g_o, g_q = pl.pallas_call(
        plain_kernel,
        out_shape=(
            jax.ShapeDtypeStruct(TOKENS, bf),
            jax.ShapeDtypeStruct(TOKENS, bf),
            jax.ShapeDtypeStruct((VROWS, D), f32),
            jax.ShapeDtypeStruct((CHUNKS, 4, 2, 2, 384, 128), bf),
            jax.ShapeDtypeStruct((CHUNKS, 4, 2, 2, 48, WIDE), bf),
            jax.ShapeDtypeStruct((4, 2, 2, 48, D), bf),
            jax.ShapeDtypeStruct((3, 4, 2, 2, 48, D), bf),
        ),
        in_specs=[ANY, ANY, SMEM, SMEM] + [ANY] * 5,
        out_specs=[ANY] * 7,
        scratch_shapes=[pltpu.VMEM(*spec) for spec in LAYER_BUFFERS.values()]
        + [pltpu.SemaphoreType.DMA((8,))],
        compiler_params=pltpu.CompilerParams(vmem_limit_bytes=63 * MIB),
    )(swap(x), swap(dy), counts, masks, w_qkv, w_o, w_up, w_dn, vecs)
    g_up = g_up.reshape(CHUNKS, D, OWNERS, 128).transpose(1, 2, 0, 3).reshape(D, FF)
    g_dn = g_dn.reshape(CHUNKS, OWNERS, D, 128).transpose(1, 0, 3, 2).reshape(FF, D)
    g_q = g_q.reshape(3, D, 3, 256).transpose(1, 2, 0, 3).reshape(D, 3 * D)

    def total(values, axis):
        share = lax.psum_scatter(values.astype(f32), "items", scatter_dimension=axis, tiled=True)
        return lax.psum(share, "blk")

    grads = [total(v, 0) for v in (g_q, g_o.reshape(D, D), g_up, g_dn)] + [total(gv[:12], 1)]
    return swap(y), swap(dx).astype(f32), grads


def body(block_input, block_cotangent, task_counts, group_mask, *states):
    masters, firsts, seconds = states[:5], states[5:10], states[10:]
    x = block_input.reshape(TOKENS)
    dy = block_cotangent.reshape(TOKENS)
    allowed = group_mask.transpose(1, 2, 0)
    if lax.axis_size("items") == OWNERS and lax.axis_size("blk") == GROUPS:
        y, dx, gv, *grads = step(x, dy, task_counts, allowed, masters)
        y, dx, new = update(masters, firsts, seconds, gv, grads, y, dx)
    else:
        y, dx, grads = plain_step(x, dy, task_counts, allowed, masters)
        parts = [
            adamw(masters[n], firsts[n], seconds[n], grads[n], rates[n], decays[n]) for n in range(5)
        ]
        new = [[part[k] for part in parts] for k in range(3)]
    return (y.reshape(block_input.shape), dx.reshape(block_input.shape), *new[0], *new[1], *new[2])


def solution(mesh):
    tokens = P("items", "blk", None, None)
    rows = P("items", None)
    state = (rows, rows, rows, rows, P(None, "items"))
    return jax.shard_map(
        body,
        mesh=mesh,
        in_specs=(tokens, tokens, P("items"), P("items", None, None)) + state * 3,
        out_specs=(tokens, tokens) + state * 3,
        check_vma=False,
    )
```

```python
import collections

import jax
import jax.numpy as jnp
from jax import lax
from jax.experimental import pallas as pl
from jax.experimental.pallas import tpu as pltpu
from jax.sharding import PartitionSpec as P

D = 768
H = 12
HD = 64
FF = 3072
GROUPS = 4
GROUP = 128
STEP = 5
CHUNKS = 3
WIDE = 1024
VROWS = 16
OWNERS = 8
MIB = 1024 * 1024

norm_eps = 1e-06
beta_one = 0.9
beta_two = 0.5
adam_eps = 1e-08
weight_decay = 0.1
rates = (0.1, 0.8, 0.1, 0.06, 1.0)
decays = (weight_decay, weight_decay, weight_decay, weight_decay, 0.0)
masked_value = -1e30

bf = jnp.bfloat16
f32 = jnp.float32
MESH = pl.DeviceIdType.MESH
ANY = pl.BlockSpec(memory_space=pl.ANY)
SMEM = pl.BlockSpec(memory_space=pltpu.SMEM)
TOKENS = (GROUPS, 2, GROUP, D)


def adamw(weight, first, second, grad, rate, decay_rate):
    first_new = beta_one * first + (1.0 - beta_one) * grad
    second_new = beta_two * second + (1.0 - beta_two) * grad * grad
    first_hat = first_new * (1.0 / (1.0 - beta_one**STEP))
    second_hat = second_new * (1.0 / (1.0 - beta_two**STEP))
    weight_new = weight - rate * (
        first_hat / (jnp.sqrt(second_hat) + adam_eps) + decay_rate * weight
    )
    return (weight_new, first_new, second_new)


def nn(a, b):
    return jnp.dot(a, b, preferred_element_type=f32)


def nt(a, b):
    return lax.dot_general(a, b, (((1,), (1,)), ((), ())), preferred_element_type=f32)


def tn(a, b):
    return lax.dot_general(a, b, (((0,), (0,)), ((), ())), preferred_element_type=f32)


def normal(values):
    mean = jnp.mean(values, -1, keepdims=True)
    centred = values - mean
    scale = lax.rsqrt(jnp.mean(centred * centred, -1, keepdims=True) + norm_eps)
    return centred * scale, scale


def norm_back(grad, normed, scale, gain):
    e = grad * gain
    along = jnp.mean(e * normed, -1, keepdims=True)
    return scale * (e - jnp.mean(e, -1, keepdims=True) - normed * along)


def rows_of(ref, g):
    block = ref[g]
    return block.reshape(2 * GROUP, block.shape[-1])


def halves(ref, k):
    block = ref[2 * k : 2 * k + 2]
    return block.reshape(512, block.shape[-1])


def put_rows(ref, g, values):
    ref[g] = values.reshape(2, GROUP, values.shape[-1])


def span256(g):
    return pl.ds(pl.multiple_of(g * 256, 256), 256)


def col_sum(values):
    return jnp.sum(values, 0, keepdims=True)


def stacked(pair, low):
    zero = jnp.zeros_like(pair)
    return jnp.concatenate([jnp.where(low, pair, zero), jnp.where(low, zero, pair)], 0)


def run_hooks(hooks, index):
    for at, hook in hooks.items():
        pl.when(index == at)(hook)


def up_block(c, i):
    lane = 3 * (i % 2) + c
    return slice(8 + i // 2, 9 + i // 2), slice(lane * 128, (lane + 1) * 128)


LAYER_BUFFERS = dict(
    x=(TOKENS, bf),
    dy=(TOKENS, bf),
    qkv=(TOKENS[:3] + (3 * D,), bf),
    o=(TOKENS, bf),
    x2=(TOKENS, f32),
    a2=(TOKENS, bf),
    a2t=((D, 1024), bf),
    dyt=((D, 1024), bf),
    gl=((1024, WIDE), bf),
    du=((1024, WIDE), bf),
    yacc=(TOKENS, f32),
    da2=(TOKENS, f32),
    dkv=((2, GROUPS * GROUP, 128), f32),
    eye=((256, 256), bf),
    stats=((H, GROUPS, 256), f32),
    vec=((VROWS, D), f32),
    bu=((CHUNKS, 1, WIDE), f32),
    gbu=((CHUNKS, 1, WIDE), f32),
    bqkv=((3, 1, D), f32),
    gv=((VROWS, D), f32),
    wqkv=((3, 4, 2, 2, 48, D), bf),
    wo=((4, 2, 2, 48, D), bf),
    wup=((CHUNKS, 4, 2, 2, 48, WIDE), bf),
    wdn=((CHUNKS, 4, 2, 2, 64, D), bf),
    gdn=((CHUNKS, 4, 2, 2, 384, 128), bf),
)


class Masks:
    def __init__(self, counts, masks):
        self.counts, self.masks, self.first = counts, masks, lax.axis_index("blk") * 2
        self.place = lax.broadcasted_iota(jnp.int32, (GROUP, 256), 0)

    def __call__(self, s, t, g):
        item = self.first + t
        open_first = self.masks[g, 0, item] * self.counts[item]
        parts = [jnp.where(self.place < open_first, s[:GROUP], masked_value)]
        for k in range(1, g + 1):
            part = s[k * GROUP : (k + 1) * GROUP]
            if k < g:
                part = part + (self.masks[g, k, item] - 1).astype(f32) * -masked_value
            parts.append(part)
        return jnp.concatenate(parts, 0)


class Layer:
    def __init__(self, refs, masks):
        self.r, self.masks = refs, masks
        self.low = lax.broadcasted_iota(jnp.int32, (1, 2 * HD), 1) < HD
        self.upper = lax.broadcasted_iota(jnp.int32, (2 * HD, 1), 0) < HD

    def start(self):
        r = self.r
        row = lax.broadcasted_iota(jnp.int32, (256, 256), 0)
        col = lax.broadcasted_iota(jnp.int32, (256, 256), 1)
        r.eye[...] = jnp.where(row == col, 1.0, 0.0).astype(bf)
        r.gv[...] = jnp.zeros_like(r.gv)
        r.gbu[...] = jnp.zeros_like(r.gbu)

    def turned(self, values):
        n = values.shape[1]
        return nt(self.r.eye[:n, :n], values).astype(bf)

    def turn_rows(self, ref, g, values):
        for m in range(3):
            ref[m * 256 : (m + 1) * 256, span256(g)] = self.turned(values[:, m * 256 : (m + 1) * 256])

    def own_heads(self, pair):
        return self.turned(jnp.where(self.upper, pair[:, :GROUP], pair[:, GROUP:]).astype(bf)).astype(bf)

    def qkv_grad(self, hq):
        return self.r.wdn.at[hq, :, :, :, pl.ds(0, 48), :]

    def vec(self, k):
        return self.r.vec[k : k + 1, :]

    def spread_biases(self):
        r = self.r
        for hq in range(3):
            for w, k in ((0, 4), (2, 5)):
                r.bqkv[hq, :, w * 256 : w * 256 + 256] = r.vec[k : k + 1, hq * 256 : hq * 256 + 256]
            r.bqkv[hq, :, 256:512] = jnp.zeros((1, 256), f32)
        for c in range(CHUNKS):
            for i in range(OWNERS):
                r.bu[c, :, i * 128 : (i + 1) * 128] = r.vec[up_block(c, i)]

    def first_norm(self, g):
        normed, _ = normal(rows_of(self.r.x, g).astype(f32))
        return (normed * self.vec(0) + self.vec(1)).astype(bf)

    def norm_item(self, t):
        r = self.r

        def step(g, _):
            normed, _ = normal(r.x[g, t].astype(f32))
            r.a2[g, t] = (normed * self.vec(0) + self.vec(1)).astype(bf)
            return 0

        lax.fori_loop(0, GROUPS, step, 0)

    def lanes(self, hq, hp, w):
        return pl.ds(pl.multiple_of(hq * D + w * 256 + hp * 128, 128), 128)

    def attend(self, part, hooks):
        r, low = self.r, self.low
        t, hq = part // 3, part % 3
        a1 = r.a2[:, t].reshape(GROUPS * GROUP, D)
        p = nn(a1, r.wqkv[hq].reshape(D, D)) + self.qkv_bias(hq)
        r.qkv[:, t, :, pl.ds(pl.multiple_of(hq * D, 128), D)] = p.astype(bf).reshape(GROUPS, GROUP, D)
        run_hooks(hooks, 3 * part)

        def step(hp, _):
            lanes = [self.lanes(hq, hp, w) for w in range(3)]
            out = pl.ds(pl.multiple_of(hq * 256 + hp * 128, 128), 128)
            k2 = r.qkv[:, t, :, lanes[1]].reshape(GROUPS * GROUP, 128)
            v2 = self.turned(r.qkv[:, t, :, lanes[2]].reshape(GROUPS * GROUP, 128))
            for g in range(GROUPS):
                n = (g + 1) * GROUP
                qs = stacked(r.qkv[g, t, :, lanes[0]] * jnp.asarray(0.125, bf), low)
                s = self.masks(nt(k2[:n], qs), t, g)
                top = jnp.max(s, 0, keepdims=True)
                e = jnp.exp(s - top)
                total = jnp.sum(e, 0, keepdims=True)
                p = (e * (1.0 / total)).astype(bf)
                r.stats[6 * t + 2 * hq + hp, g : g + 1, :] = top + jnp.log(total)
                r.o[g, t, :, out] = self.own_heads(nn(v2[:, :n], p))
            run_hooks(hooks, 3 * part + 1 + hp)
            return 0

        lax.fori_loop(0, 2, step, 0)

    def qkv_bias(self, hq):
        return self.r.bqkv[hq]

    def middle(self, hooks):
        r = self.r

        def step(g, _):
            v = rows_of(r.x, g).astype(f32) + nn(rows_of(r.o, g), r.wo[...].reshape(D, D)) + self.vec(6)
            put_rows(r.x2, g, v)
            put_rows(r.yacc, g, v + self.vec(7))
            normed, _ = normal(v)
            a = (normed * self.vec(2) + self.vec(3)).astype(bf)
            put_rows(r.a2, g, a)
            self.turn_rows(r.a2t, g, a)
            dy = rows_of(r.dy, g)
            self.turn_rows(r.dyt, g, dy)
            put_rows(r.da2, g, jnp.zeros((256, D), f32))
            r.gv[7:8, :] += col_sum(dy.astype(f32))
            run_hooks(hooks, g)
            return 0

        lax.fori_loop(0, GROUPS, step, 0)

    def feed(self, hooks):
        r = self.r

        def column(c, j):
            cols = span256(j)
            wup = r.wup[c, :, :, :, :, cols].reshape(D, 256)
            wdn = r.wdn[c, j].reshape(256, D)
            for k in range(2):
                rows = slice(512 * k, 512 * k + 512)
                u = nn(halves(r.a2, k), wup) + r.bu[c, :, cols]
                u2 = u * u
                half = 0.5 * jnp.tanh(u * (0.7978845608028654 + 0.035677408136300125 * u2)) + 0.5
                r.gl[rows, cols] = (u * half).astype(bf)
                slope = half + u * (2.0 * half * (1.0 - half)) * (
                    0.7978845608028654 + 0.10703222440890037 * u2
                )
                d = (nt(halves(r.dy, k), wdn) * slope).astype(bf)
                r.du[rows, cols] = d
                r.gbu[c, :, cols] += col_sum(d.astype(f32))

        def chunk(c, _):
            def step(j, _):
                column(c, j)
                run_hooks(hooks, 10 * c + j)
                return 0

            def down_grad(h, _):
                down = nn(r.dyt[pl.ds(pl.multiple_of(h * 384, 384), 384), :], r.gl[...]).astype(bf)
                for i in range(OWNERS):
                    r.gdn[c, i // 2, i % 2, h] = down[:, i * 128 : (i + 1) * 128]
                return 0

            def up_back(k, _):
                rows = pl.ds(pl.multiple_of(512 * k, 512), 512)
                back = nt(r.du[rows, :], r.wup[c].reshape(D, WIDE))
                r.da2[pl.ds(2 * k, 2)] += back.reshape(2, 2, GROUP, D)
                return 0

            def up_grad(h, _):
                up = nn(r.a2t[pl.ds(pl.multiple_of(h * 384, 384), 384), :], r.du[...]).astype(bf)
                r.wup[c, pl.ds(2 * h, 2)] = up.reshape(2, 2, 2, 48, WIDE)
                return 0

            def down(k, _):
                rows = pl.ds(pl.multiple_of(512 * k, 512), 512)
                out = nn(r.gl[rows, :], r.wdn[c].reshape(WIDE, D))
                r.yacc[pl.ds(2 * k, 2)] += out.reshape(2, 2, GROUP, D)
                return 0

            lax.fori_loop(0, 4, step, 0)
            for n, act in enumerate((down_grad, up_back, up_grad, down)):
                lax.fori_loop(0, 2, act, 0)
                run_hooks(hooks, 10 * c + 4 + n)
            return 0

        lax.fori_loop(0, CHUNKS, chunk, 0)
        for c in range(CHUNKS):
            for i in range(OWNERS):
                r.gv[up_block(c, i)] = r.gbu[c, :, i * 128 : (i + 1) * 128]

    def turn(self, order, send, hooks):
        r = self.r

        def step(k, _):
            g = order(k)
            c = rows_of(r.da2, g)
            normed, scale = normal(rows_of(r.x2, g))
            r.gv[2:3, :] += col_sum(c * normed)
            r.gv[3:4, :] += col_sum(c)
            d = rows_of(r.dy, g).astype(f32) + norm_back(c, normed, scale, self.vec(2))
            put_rows(r.dy, g, rows_of(r.yacc, g).astype(bf))
            send(k, g)
            put_rows(r.da2, g, d)
            r.gv[6:7, :] += col_sum(d)
            dz = d.astype(bf)
            put_rows(r.a2, g, dz)
            self.turn_rows(r.gl, g, rows_of(r.o, g))
            self.turn_rows(r.du, g, self.first_norm(g))
            put_rows(r.yacc, g, jnp.zeros((256, D), f32))
            run_hooks(hooks, k)
            return 0

        lax.fori_loop(0, GROUPS, step, 0)

    def out_grads(self):
        r = self.r

        def back(k, _):
            rows = pl.ds(2 * k, 2)
            do = nt(r.a2[rows].reshape(512, D), r.wo[...].reshape(D, D)).astype(bf)
            r.o[rows] = do.reshape(2, 2, GROUP, D)
            return 0

        def grad(h, _):
            part = r.gl[pl.ds(pl.multiple_of(h * 384, 384), 384), :]
            grads = nn(part, r.a2[...].reshape(GROUPS * 256, D)).astype(bf)
            r.wo[pl.ds(2 * h, 2)] = grads.reshape(2, 2, 2, 48, D)
            return 0

        lax.fori_loop(0, 2, back, 0)
        lax.fori_loop(0, 2, grad, 0)

    def attend_back(self, hooks, order, send):
        r, low = self.r, self.low

        def pair(hq, t, hp):
            lanes = [self.lanes(hq, hp, w) for w in range(3)]
            out = pl.ds(pl.multiple_of(hq * 256 + hp * 128, 128), 128)
            r.dkv[...] = jnp.zeros_like(r.dkv)
            k2 = r.qkv[:, t, :, lanes[1]].reshape(GROUPS * GROUP, 128)
            v2 = r.qkv[:, t, :, lanes[2]].reshape(GROUPS * GROUP, 128)
            turned_k = self.turned(k2)
            for g in range(GROUPS):
                n = (g + 1) * GROUP
                qs = stacked(r.qkv[g, t, :, lanes[0]] * jnp.asarray(0.125, bf), low)
                dos = stacked(r.o[g, t, :, out], low)
                s = self.masks(nt(k2[:n], qs), t, g)
                p = jnp.exp(s - r.stats[6 * t + 2 * hq + hp, g : g + 1, :])
                dp = nt(v2[:n], dos)
                ds = (p * (dp - jnp.sum(p * dp, 0, keepdims=True))).astype(bf)
                r.dkv[0, :n, :] += nn(ds, qs)
                r.dkv[1, :n, :] += nn(p.astype(bf), dos)
                r.qkv[g, t, :, lanes[0]] = self.own_heads(nn(turned_k[:, :n], ds) * 0.125)
            for w in range(2):
                r.qkv[:, t, :, lanes[w + 1]] = r.dkv[w].astype(bf).reshape(GROUPS, GROUP, 128)

        def quad(hq, _):
            cols = pl.ds(pl.multiple_of(hq * D, 128), D)

            def item(t, _):
                def step(hp, _):
                    pair(hq, t, hp)
                    run_hooks(hooks, 10 * hq + 2 * t + hp)
                    return 0

                lax.fori_loop(0, 2, step, 0)
                pl.when(t == 1)(lambda: grads(hq, cols))
                run_hooks(hooks, 10 * hq + 4 + t)
                rows = r.qkv[:, t, :, cols].reshape(512, D)
                back = nt(rows, r.wqkv[hq].reshape(D, D))
                r.yacc[:, t] += back.reshape(GROUPS, GROUP, D)
                run_hooks(hooks, 10 * hq + 6 + t)

                @pl.when(hq == 2)
                def _():
                    lax.fori_loop(0, GROUPS, lambda k, _: finish(t, k), 0)
                    run_hooks(hooks, 10 * hq + 8 + t)

                return 0

            lax.fori_loop(0, 2, item, 0)
            return 0

        def grads(hq, cols):
            d = r.qkv[:, :, :, cols].reshape(GROUPS * 256, D)

            def grad(h, _):
                part = r.du[pl.ds(pl.multiple_of(h * 384, 384), 384), :]
                out = nn(part, d).astype(bf)
                r.wdn[hq, pl.ds(2 * h, 2), :, :, :48, :] = out.reshape(2, 2, 2, 48, D)
                return 0

            lax.fori_loop(0, 2, grad, 0)
            sums = col_sum(d.astype(f32))
            r.gv[4:5, span256(hq)] = sums[:, :256]
            r.gv[5:6, span256(hq)] = sums[:, 512:]

        def finish(t, k):
            g = order(k)
            c = r.yacc[g, t]
            normed, scale = normal(r.x[g, t].astype(f32))
            r.gv[0:1, :] += col_sum(c * normed)
            r.gv[1:2, :] += col_sum(c)
            d = r.da2[g, t] + norm_back(c, normed, scale, self.vec(0))
            r.x[g, t] = d.astype(bf)
            send(k, t)
            return 0

        lax.fori_loop(0, 3, quad, 0)


class Here:
    def __init__(self):
        self.i, self.b = lax.axis_index("items"), lax.axis_index("blk")
        self.z, self.y = self.i // 2, self.i % 2
        self.x, self.c = self.b // 2, self.b % 2

    def z_plus(self, k):
        return (self.z + k) % 4

    def at_z(self, k):
        return (2 * self.z_plus(k) + self.y, self.b)

    def at_y(self):
        return (self.i + 1 - 2 * self.y, self.b)

    def at_x(self):
        return (self.i, (self.b + 2) % 4)

    def at_core(self):
        return (self.i, self.b + 1 - 2 * self.c)

    def at_blk(self, k):
        return (self.i, (self.b + k) % 4)

    def at_items(self, k):
        return ((self.i + k) % OWNERS, self.b)


def remote(src, dst, send, recv, device):
    return pltpu.make_async_remote_copy(
        src_ref=src, dst_ref=dst, send_sem=send, recv_sem=recv, device_id=device, device_id_type=MESH
    )


class Mail:
    def __init__(self, here, send, recv):
        self.here, self.send, self.recv = here, send, recv

    def go(self, src, dst, slot, device):
        remote(src, dst, self.send.at[slot], self.recv.at[slot], device).start()

    def arrived(self, dst, slot):
        remote(dst, dst, self.send.at[slot], self.recv.at[slot], self.here.at_core()).wait_recv()

    def left(self, src, *slots):
        for slot in slots:
            remote(src, src, self.send.at[slot], self.recv.at[slot], self.here.at_core()).wait_send()


class Gather(Mail):
    slots = 5

    def __init__(self, here, dst, send, recv):
        super().__init__(here, send, recv)
        self.dst = dst

    def first(self):
        h = self.here
        own = self.dst.at[h.z, h.y, h.c]
        for k in (1, 2, 3):
            self.go(own, own, k - 1, h.at_z(k))

    def second(self):
        h = self.here
        for k in (1, 2, 3):
            self.arrived(self.dst.at[h.z_plus(4 - k), h.y, h.c], k - 1)
        line = self.dst.at[:, h.y, h.c]
        self.go(line, line, 3, h.at_y())

    def third(self):
        h = self.here
        self.arrived(self.dst.at[:, 1 - h.y, h.c], 3)
        half = self.dst.at[:, :, h.c]
        self.go(half, half, 4, h.at_core())

    def last(self):
        self.arrived(self.dst.at[:, :, 1 - self.here.c], 4)

    def drain(self):
        self.left(self.dst.at[0, 0, 0], 0, 1, 2)
        self.left(self.dst.at[:, 0, 0], 3)
        self.left(self.dst.at[:, :, 0], 4)


class SplitGather(Gather):
    slots = 6

    def mine(self, z, y):
        h = self.here
        return self.dst.at[z, y, h.c, :, self.columns(h.x)]

    def columns(self, x):
        width = self.dst.shape[-1] // 2
        return pl.ds(pl.multiple_of(x * width, width), width)

    def first(self):
        h = self.here
        own = self.mine(h.z, h.y)
        for k in (1, 2, 3):
            self.go(own, own, k - 1, h.at_z(k))

    def second(self):
        h = self.here
        for k in (1, 2, 3):
            self.arrived(self.mine(h.z_plus(4 - k), h.y), k - 1)
        line = self.mine(slice(None), h.y)
        self.go(line, line, 3, h.at_y())

    def across(self):
        h = self.here
        self.arrived(self.mine(slice(None), 1 - h.y), 3)
        part = self.mine(slice(None), slice(None))
        self.go(part, part, 5, h.at_x())

    def third(self):
        h = self.here
        self.arrived(self.dst.at[:, :, h.c, :, self.columns(1 - h.x)], 5)
        half = self.dst.at[:, :, h.c]
        self.go(half, half, 4, h.at_core())

    def drain(self):
        self.left(self.mine(0, 0), 0, 1, 2)
        self.left(self.mine(slice(None), 0), 3)
        self.left(self.dst.at[:, :, 0], 4)
        self.left(self.mine(slice(None), slice(None)), 5)


class Exchange(Mail):
    def __init__(self, here, src, dst, send, recv, local):
        super().__init__(here, send, recv)
        self.src, self.dst, self.local = src, dst, local

    def own(self):
        h = self.here
        return pltpu.make_async_copy(self.src.at[h.b], self.dst.at[h.b], self.local)

    def order(self, k):
        h = self.here
        odd, near = k % 2, k // 2
        far = (1 - odd) * ((h.b + 2) % 4) + odd * (3 - h.b)
        return (1 - near) * far + near * (h.b + (1 - odd) * (1 - 2 * h.c))

    def copy(self, k):
        h = self.here
        to = self.order(k)
        return remote(self.src.at[to], self.dst.at[h.b], self.send.at[k], self.recv.at[k], (h.i, to))

    def put(self, k, _=None):
        @pl.when(k < 3)
        def _():
            self.copy(k).start()

        @pl.when(k == 3)
        def _():
            self.own().start()

    def start(self):
        for k in range(3):
            self.copy(k).start()
        self.own().start()

    def arrive(self):
        self.own().wait()
        for k in range(3):
            self.arrived(self.dst.at[self.order(k)], k)

    def drain(self):
        for k in range(3):
            self.copy(k).wait_send()


class ItemExchange(Exchange):
    def copy(self, k, t):
        h = self.here
        to, slot = self.order(k), 3 * t + k
        return remote(
            self.src.at[to, t], self.dst.at[h.b, t], self.send.at[slot], self.recv.at[slot], (h.i, to)
        )

    def own(self, t):
        h = self.here
        return pltpu.make_async_copy(self.src.at[h.b, t], self.dst.at[h.b, t], self.local.at[t])

    def put(self, k, t):
        @pl.when(k < 3)
        def _():
            self.copy(k, t).start()

        @pl.when(k == 3)
        def _():
            self.own(t).start()

    def start(self, t):
        for k in range(3):
            self.copy(k, t).start()
        self.own(t).start()

    def arrive(self, t):
        self.own(t).wait()
        for k in range(3):
            self.arrived(self.dst.at[self.order(k), t], 3 * t + k)

    def drain(self):
        self.left(self.src.at[0, 0], *range(6))


class Reduce(Mail):
    slots = 8

    def __init__(self, here, g, rc, place, count, credit, ry, rz, rx, total, out, send, recv):
        super().__init__(here, send, recv)
        self.g, self.rc, self.place, self.count, self.credit = g, rc, place, count, credit
        self.ry, self.rz, self.rx, self.total, self.out = ry, rz, rx, total, out

    def over_core(self):
        h = self.here
        if self.place is not None and self.place >= 2:
            pl.semaphore_wait(self.credit, 1)
        self.go(self.g.at[:, :, 1 - h.c], self.rc, 0, h.at_core())

    def over_y(self):
        h = self.here
        self.arrived(self.rc, 0)

        def add(n, _):
            z, y = n // 2, n % 2
            self.g[z, y, h.c] = self.g[z, y, h.c] + self.rc[z, y]
            return 0

        lax.fori_loop(0, 8, add, 0)
        if self.place is not None and self.place + 2 < self.count:
            pl.semaphore_signal(self.credit, inc=1, device_id=h.at_core(), device_id_type=MESH)
        self.go(self.g.at[:, 1 - h.y, h.c], self.ry, 1, h.at_y())

    def over_z(self):
        h = self.here
        self.arrived(self.ry, 1)

        def add(z, _):
            self.g[z, h.y, h.c] = self.g[z, h.y, h.c] + self.ry[z]
            return 0

        lax.fori_loop(0, 4, add, 0)
        for k in (2, 1, 3):
            self.go(self.g.at[h.z_plus(k), h.y, h.c], self.rz.at[k - 1], 1 + k, h.at_z(k))

    def over_x(self):
        h = self.here
        part = self.g[h.z, h.y, h.c].astype(f32)
        for k in (1, 2, 3):
            self.arrived(self.rz.at[k - 1], 1 + k)
            part = part + self.rz[k - 1].astype(f32)
        self.total[0] = part.astype(bf)
        self.go(self.total.at[0], self.rx, 5, h.at_x())

    def share(self):
        h = self.here
        self.arrived(self.rx, 5)
        self.total[1] = self.total[0] + self.rx[...]
        self.own().start()
        self.go(self.total.at[1], self.out.at[h.c], 6, h.at_core())

    def own(self):
        return pltpu.make_async_copy(self.total.at[1], self.out.at[self.here.c], self.send.at[7])

    def last(self):
        self.arrived(self.out.at[1 - self.here.c], 6)
        self.own().wait()

    def drain(self):
        self.left(self.rc, 0)
        self.left(self.ry, 1)
        self.left(self.rz.at[0], 2, 3, 4)
        self.left(self.rx, 5, 6)


class SplitReduce(Reduce):
    slots = 9

    def __init__(self, rx0, *args):
        super().__init__(*args)
        self.rx0 = rx0

    def rows(self, x):
        count = self.g.shape[-2] // 2
        return pl.ds(pl.multiple_of(x * count, count), count)

    def over_x0(self):
        h = self.here
        self.arrived(self.rc, 0)

        def add(n, _):
            z, y = n // 2, n % 2
            self.g[z, y, h.c] = self.g[z, y, h.c] + self.rc[z, y]
            return 0

        lax.fori_loop(0, 8, add, 0)
        if self.place + 2 < self.count:
            pl.semaphore_signal(self.credit, inc=1, device_id=h.at_core(), device_id_type=MESH)
        self.go(self.g.at[:, :, h.c, self.rows(1 - h.x)], self.rx0, 8, h.at_x())

    def over_y(self):
        h = self.here
        mine = self.rows(h.x)
        self.arrived(self.rx0, 8)

        def add(n, _):
            z, y = n // 2, n % 2
            self.g[z, y, h.c, mine] = self.g[z, y, h.c, mine] + self.rx0[z, y]
            return 0

        lax.fori_loop(0, 8, add, 0)
        self.go(self.g.at[:, 1 - h.y, h.c, mine], self.ry.at[:, self.rows(0)], 1, h.at_y())

    def over_z(self):
        h = self.here
        mine, box = self.rows(h.x), self.rows(0)
        self.arrived(self.ry.at[:, box], 1)

        def add(z, _):
            self.g[z, h.y, h.c, mine] = self.g[z, h.y, h.c, mine] + self.ry[z, box]
            return 0

        lax.fori_loop(0, 4, add, 0)
        for k in (2, 1, 3):
            self.go(self.g.at[h.z_plus(k), h.y, h.c, mine], self.rz.at[k - 1, box], 1 + k, h.at_z(k))

    def over_x(self):
        h = self.here
        mine, box = self.rows(h.x), self.rows(0)
        part = self.g[h.z, h.y, h.c, mine].astype(f32)
        for k in (1, 2, 3):
            self.arrived(self.rz.at[k - 1, box], 1 + k)
            part = part + self.rz[k - 1, box].astype(f32)
        self.total[1, mine] = part.astype(bf)
        done = self.total.at[1, mine]
        self.go(done, done, 5, h.at_x())

    def share(self):
        h = self.here
        self.arrived(self.total.at[1, self.rows(1 - h.x)], 5)
        self.own().start()
        self.go(self.total.at[1], self.out.at[h.c], 6, h.at_core())

    def drain(self):
        box = self.rows(0)
        self.left(self.rc, 0)
        self.left(self.ry.at[:, box], 1)
        self.left(self.rz.at[0, box], 2, 3, 4)
        self.left(self.total.at[1, box], 5)
        self.left(self.rx, 6)
        self.left(self.rx0, 8)


WINDOW = 256


def window_start(owner):
    return (3 * owner // 4 - owner // 7) * 128


def window_of(owner):
    return pl.ds(pl.multiple_of(window_start(owner), 128), WINDOW)


class ReduceVectors(Mail):
    def __init__(self, here, v, blk_inbox, items_inbox, out, send, recv):
        super().__init__(here, send, recv)
        self.v, self.blk_inbox, self.items_inbox, self.out = v, blk_inbox, items_inbox, out

    def first(self):
        h = self.here
        self.blk_inbox[h.b] = self.v[...]
        for k in (1, 2, 3):
            self.go(self.v, self.blk_inbox.at[h.b], k - 1, h.at_blk(k))

    def second(self):
        h = self.here
        for k in (1, 2, 3):
            self.arrived(self.blk_inbox.at[(h.b + 4 - k) % 4], k - 1)
        self.left(self.v, 0, 1, 2)
        box = self.blk_inbox
        self.v[...] = (box[0] + box[1]) + (box[2] + box[3])
        for k in range(1, OWNERS):
            owner = (h.i + k) % OWNERS
            self.go(
                self.v.at[:, window_of(owner)], self.items_inbox.at[h.i], 2 + k, h.at_items(k)
            )
        self.items_inbox[h.i] = self.v[:, window_of(h.i)]

    def third(self):
        h = self.here
        for k in range(1, OWNERS):
            self.arrived(self.items_inbox.at[(h.i + OWNERS - k) % OWNERS], 2 + k)
        total = self.items_inbox[0]
        for n in range(1, OWNERS):
            total = total + self.items_inbox[n]
        self.out[...] = total

    def drain(self):
        self.left(self.out, *range(3, 10))


INBOXES = (("d", CHUNKS, 384, 128), ("u", CHUNKS, 48, WIDE), ("q", 4, 48, D))
COMM_BUFFERS = dict(
    rcd=((2, 4, 2, 384, 128), bf),
    rcu=((2, 4, 2, 48, WIDE), bf),
    vbox=((OWNERS, VROWS, WINDOW), bf),
    gbox=((GROUPS, VROWS, D), f32),
    wbox=((OWNERS, VROWS, WINDOW), f32),
    gvw=((VROWS, WINDOW), f32),
    wvec=((12, 96), f32),
    rx0=((2, 4, 2, 192, 128), bf),
)
for _kind, _n, _rows, _cols in INBOXES:
    COMM_BUFFERS["ry" + _kind] = ((_n, 4, _rows, _cols), bf)
    COMM_BUFFERS["rz" + _kind] = ((_n, 3, _rows, _cols), bf)
    COMM_BUFFERS["rx" + _kind] = ((_n, _rows, _cols), bf)
    COMM_BUFFERS["tt" + _kind] = ((_n, 2, _rows, _cols), bf)
SEMS = dict(
    load=(12,),
    gsend=(12, SplitGather.slots),
    grecv=(12, SplitGather.slots),
    rsend=(12, SplitReduce.slots),
    rrecv=(12, SplitReduce.slots),
    xsend=(2, 6),
    xrecv=(2, 6),
    xlocal=(2, 2),
    esend=(2, 3),
    erecv=(2, 3),
    local=(5,),
    vsend=(7,),
    vrecv=(7,),
    wsend=(10,),
    wrecv=(10,),
)


SPLIT_DOWN = (1, 2)
MOVES = dict(
    a="first", l="second", xx="across", h="third", w="last",
    core="over_core", x0="over_x0", y="over_y", z="over_z", x="over_x", sh="share", end="last",
)
TIMETABLE = dict(
    start=(("Q0q", "a"), ("Q0k", "a"), ("Q0v", "a"),),
    table=(("Q0q", "l"), ("Q0k", "l"), ("Q1", "a"), ("Q0q", "h"), ("Q0v", "l"), ("Q2", "a"), ("Q0k", "h"), ("Q0q", "w"),),
    ln0=(("Q0v", "h"), ("Q0k", "w"), ("Q0v", "w"),),
    s0a=(("Q1", "l"), ("O", "a"),),
    s0b=(("Q2", "l"), ("U0", "a"), ("Q1", "h"), ("Q1", "w"),),
    s1p=(("O", "l"), ("D0", "a"),),
    s1b=(("Q2", "h"), ("U0", "l"), ("U1", "a"), ("Q2", "w"),),
    s2a=(("O", "h"),),
    s3a=(("O", "w"), ("U0", "xx"), ("D0", "l"), ("D1", "a"),),
    s4b=(("U1", "l"), ("U2", "a"),),
    m1=(("U0", "h"), ("D0", "h"),),
    m3=(("D1", "l"), ("D2", "a"), ("U0", "w"), ("U1", "xx"), ("D0", "w"),),
    f00=(("U2", "l"),),
    f03=(("D1", "h"),),
    g00=(("U1", "h"), ("d0", "core"),),
    g01=(("D1", "w"), ("U2", "xx"), ("D2", "l"),),
    g02=(("U1", "w"), ("u0", "core"),),
    f10=(("d0", "y"),),
    f11=(("u0", "y"),),
    f13=(("U2", "h"), ("D2", "h"),),
    g10=(("d1", "core"),),
    g11=(("U2", "w"),),
    g12=(("u1", "core"),),
    g13=(("D2", "w"), ("d0", "z"),),
    f20=(("d1", "x0"),),
    f21=(("u1", "y"),),
    g20=(("u0", "z"), ("d2", "core"),),
    g21=(("d0", "x"),),
    g22=(("d1", "y"), ("d2", "x0"), ("u2", "core"),),
    g23=(("d0", "sh"),),
    t1=(("u1", "z"), ("u2", "y"), ("d0", "end"),),
    t3=(("u0", "x"),),
    gwo=(("d1", "z"), ("o", "core"),),
    b00=(("d2", "y"),),
    b01=(("o", "y"),),
    b02=(("u1", "x"),),
    b03=(("u2", "z"),),
    gq0=(("d1", "x"), ("q0", "core"),),
    b10=(("d2", "z"),),
    b11=(("q0", "y"),),
    b13=(("o", "z"), ("u2", "x"),),
    gq1=(("q1", "core"),),
    on11=(("u0", "sh"),),
    b20=(("u1", "sh"), ("d2", "x"),),
    b21=(("u0", "end"), ("d1", "sh"), ("u1", "end"), ("q0", "z"), ("q1", "y"),),
    on20=(("u2", "sh"), ("d1", "end"),),
    fin0=(("d2", "sh"),),
    b22=(("u2", "end"), ("o", "x"), ("d2", "end"),),
    gq2=(("q2q", "core"), ("q2k", "core"), ("q2v", "core"),),
    on21=(("q1", "z"),),
    fin1=(("q2q", "y"), ("q2k", "y"), ("q0", "x"),),
    tail0=(("q2v", "y"), ("o", "sh"), ("q2q", "z"), ("o", "end"), ("q2k", "z"), ("q1", "x"), ("q2v", "z"), ("q2q", "x"), ("q2k", "x"), ("q0", "sh"), ("q2v", "x"),),
    tail1=(("q0", "end"), ("q1", "sh"), ("q2q", "sh"), ("q2k", "sh"), ("q2v", "sh"), ("q1", "end"), ("q2q", "end"),),
    tail2=(("q2k", "end"), ("q2v", "end"),),
)


def step_kernel(*refs):
    (xs, dys, counts, masks, w_qkv, w_o, w_up, w_dn, w_vec, y, dx, gv, o_dn, o_up, o_o, o_q) = refs[:16]
    names = list(LAYER_BUFFERS) + list(COMM_BUFFERS) + list(SEMS) + ["credit_d", "credit_u"]
    r = collections.namedtuple("Refs", names)(*refs[16:])
    here = Here()
    barrier = pltpu.get_barrier_semaphore()
    friends = [here.at_items(k) for k in range(1, OWNERS)] + [here.at_blk(k) for k in (1, 2, 3)]
    for device in friends:
        pl.semaphore_signal(barrier, inc=1, device_id=device, device_id_type=MESH)

    half = pl.ds(here.c * 48, 48)
    small, small_dn = pl.ds(0, 48), pl.ds(0, 64)
    loads = []
    for q in range(3):
        loads.append((w_qkv.at[half, pl.ds(q * D, D)], r.x2.at[q // 2, q % 2, small, :]))
    loads.append((w_o.at[half], r.x2.at[1, 1, small, :]))
    for q in range(4):
        loads.append((w_up.at[half, pl.ds(q * D, D)], r.x2.at[2 + q // 2, q % 2, small, :]))
    for q in range(3):
        rows = pl.ds(q * 128 + here.c * 64, 64)
        loads.append((w_dn.at[rows], r.yacc.at[q // 2, q % 2, small_dn, :]))
    loads.append((w_vec, r.wvec))
    loads = [pltpu.make_async_copy(s, d, r.load.at[n]) for n, (s, d) in enumerate(loads)]
    for load in loads:
        load.start()

    layer = Layer(r, Masks(counts, masks))
    pl.semaphore_wait(barrier, len(friends))

    x_in = ItemExchange(here, xs, r.x, r.xsend.at[0], r.xrecv.at[0], r.xlocal.at[0])
    dy_in = Exchange(here, dys, r.dy, r.esend.at[0], r.erecv.at[0], r.local.at[1])
    y_out = Exchange(here, r.dy, y, r.esend.at[1], r.erecv.at[1], r.local.at[2])
    dx_out = ItemExchange(here, r.x, dx, r.xsend.at[1], r.xrecv.at[1], r.xlocal.at[1])

    count = iter(range(12))

    def gather(dst, parts, kind=Gather):
        width = dst.shape[-1] // parts
        units = []
        for p in range(parts):
            n = next(count)
            part = dst.at[:, :, :, :, pl.ds(p * width, width)]
            units.append(kind(here, part, r.gsend.at[n], r.grecv.at[n]))
        return units

    g_q = [gather(r.wqkv.at[hq], 1 if hq else 3) for hq in range(3)]
    (g_o,) = gather(r.wo, 1)
    g_u = [gather(r.wup.at[c], 1, SplitGather) for c in range(CHUNKS)]
    g_d = [gather(r.wdn.at[c], 1) for c in range(CHUNKS)]

    def reduce(kind, n, index, g, rc, place, count, credit, out):
        boxes = [getattr(r, box + kind).at[n] for box in ("ry", "rz", "rx", "tt")]
        args = (here, g, rc, place, count, credit, *boxes, out, r.rsend.at[index], r.rrecv.at[index])
        if kind == "d" and n in SPLIT_DOWN:
            return SplitReduce(r.rx0.at[n - 1], *args)
        return Reduce(*args)

    s_d = [
        reduce("d", c, 2 * c, r.gdn.at[c], r.rcd.at[c % 2], c, 3, r.credit_d, o_dn.at[c])
        for c in range(CHUNKS)
    ]
    s_u = [
        reduce("u", c, 2 * c + 1, r.wup.at[c], r.rcu.at[c % 2], c, 7, r.credit_u, o_up.at[c])
        for c in range(CHUNKS)
    ]
    narrow = [r.rcu.at[n % 2, :, :, :, pl.ds(0, D)] for n in range(2)]
    s_o = reduce("q", 3, 6, r.wo, narrow[1], 3, 7, r.credit_u, o_o)
    s_q = [
        reduce("q", c, 7 + c, layer.qkv_grad(c), narrow[c % 2], 4 + c, 7, r.credit_u, o_q.at[c])
        for c in range(2)
    ]
    for w in range(3):
        third = pl.ds(256 * w, 256)
        boxes = [r.ryq.at[2, :, :, third], r.rzq.at[2, :, :, third], r.rxq.at[2, :, third], r.ttq.at[2, :, :, third]]
        s_q.append(
            Reduce(
                here, r.wdn.at[2, :, :, :, pl.ds(0, 48), third], r.rcu.at[0, :, :, :, third],
                6 if w == 0 else None, 7, r.credit_u, *boxes, o_q.at[2, :, :, third],
                r.rsend.at[9 + w], r.rrecv.at[9 + w],
            )
        )
    sums = ReduceVectors(here, r.gv, r.gbox, r.wbox, r.gvw, r.wsend, r.wrecv)

    units = {"O": g_o, "o": s_o, "q0": s_q[0], "q1": s_q[1]}
    for c in range(CHUNKS):
        units |= {f"d{c}": s_d[c], f"u{c}": s_u[c]}
        for base, parts in (("Q", g_q[c]), ("U", g_u[c]), ("D", g_d[c])):
            names = ("q", "k", "v") if len(parts) > 1 else ("",)
            units |= {f"{base}{c}{name}": part for name, part in zip(names, parts)}
    units |= {f"q2{name}": part for name, part in zip("qkv", s_q[2:])}

    def at(slot):
        for unit, name in TIMETABLE.get(slot, ()):
            getattr(units[unit], MOVES[name])()

    def slots(**names):
        return {
            index: (lambda slot=slot: at(slot)) for slot, index in names.items() if slot in TIMETABLE
        }

    x_in.start(0)
    for q in range(3):
        loads[q].wait()
        part = r.x2[q // 2, q % 2, :48, :].astype(bf)
        for hq in range(3):
            r.wqkv[hq, here.z, here.y, here.c, :, q * 256 : q * 256 + 256] = part[:, hq * 256 : hq * 256 + 256]
    at("start")
    at("more")

    rows = lax.broadcasted_iota(jnp.int32, (96, WINDOW), 0)
    cols = lax.broadcasted_iota(jnp.int32, (96, WINDOW), 1)
    chosen = jnp.where(cols - (here.i * 96 - window_start(here.i)) == rows, 1.0, 0.0).astype(bf)
    loads[11].wait()
    r.vbox[here.i] = jnp.concatenate(
        [nn(r.wvec[...].astype(bf), chosen), jnp.zeros((VROWS - 12, WINDOW), f32)], 0
    ).astype(bf)
    table = Mail(here, r.vsend, r.vrecv)
    for k in range(1, OWNERS):
        own = r.vbox.at[here.i]
        table.go(own, own, k - 1, here.at_items(k))
    layer.start()
    loads[3].wait()
    r.wo[here.z, here.y, here.c] = r.x2[1, 1, :48, :].astype(bf)
    for q in range(4):
        loads[4 + q].wait()
        part = r.x2[2 + q // 2, q % 2, :48, :].astype(bf)
        for m in range(6):
            i, c = (6 * q + m) // 3, (6 * q + m) % 3

            @pl.when(here.x == i // 4)
            def _(i=i, c=c, part=part[:, m * 128 : (m + 1) * 128]):
                r.wup[c, here.z, here.y, here.c, :, i * 128 : (i + 1) * 128] = part

    for c in range(CHUNKS):
        loads[8 + c].wait()
        r.wdn[c, here.z, here.y, here.c] = r.yacc[c // 2, c % 2, :64, :].astype(bf)

    at("cast")
    for k in range(1, OWNERS):
        table.arrived(r.vbox.at[(here.i + OWNERS - k) % OWNERS], k - 1)
    r.vec[...] = jnp.zeros_like(r.vec)
    for n in range(OWNERS):
        start = window_start(n)
        r.vec[:, start : start + WINDOW] += r.vbox[n].astype(f32)
    layer.spread_biases()
    at("table")
    x_in.arrive(0)
    x_in.start(1)
    layer.norm_item(0)
    at("ln0")

    def other_item():
        x_in.arrive(1)
        layer.norm_item(1)

    in_parts = slots(**{f"s{n}{'pab'[j]}": 3 * n + j for n in range(6) for j in range(3)})
    for index, extra in ((2, dy_in.start), (8, other_item)):

        def both(before=in_parts.get(index, lambda: None), extra=extra):
            before()
            extra()

        in_parts[index] = both

    def part(n, _):
        layer.attend(n, in_parts)
        return 0

    lax.fori_loop(0, 6, part, 0)
    dy_in.arrive()
    at("dy")
    layer.middle(slots(**{f"m{k}": k for k in range(GROUPS)}))
    in_feed = {f"f{c}{j}": 10 * c + j for c in range(CHUNKS) for j in range(4)}
    in_feed |= {f"g{c}{n}": 10 * c + 4 + n for c in range(CHUNKS) for n in range(4)}
    in_feed = slots(**in_feed)
    for c in range(CHUNKS):

        def overwrite(c=c, before=in_feed.get(10 * c + 5, lambda: None)):
            before()
            for part in g_u[c]:
                part.drain()

        in_feed[10 * c + 5] = overwrite
    layer.feed(in_feed)
    dy_in.drain()
    layer.turn(y_out.order, y_out.put, slots(**{f"t{k}": k for k in range(GROUPS)}))
    g_o.drain()
    for part in g_d[0] + g_d[1] + g_d[2]:
        part.drain()
    layer.out_grads()
    at("gwo")
    in_back = {f"b{q}{k}": 10 * q + k for q in range(3) for k in range(4)}
    in_back |= {f"gq{q}": 10 * q + 5 for q in range(3)}
    in_back |= {f"on{q}{t}": 10 * q + 6 + t for q in range(3) for t in range(2)}
    in_back |= {f"fin{t}": 28 + t for t in range(2)}
    layer.attend_back(slots(**in_back), dx_out.order, dx_out.put)
    sums.first()
    y_out.arrive()
    for part in g_q[0] + g_q[1] + g_q[2] + [x_in, y_out]:
        part.drain()
    table.left(r.vbox.at[0], *range(OWNERS - 1))
    at("tail0")
    sums.second()
    for part in s_d + s_u + [s_o]:
        part.drain()
    at("tail1")
    sums.third()
    store = pltpu.make_async_copy(r.gvw, gv, r.local.at[4])
    store.start()
    at("tail2")
    dx_out.arrive(0)
    dx_out.arrive(1)
    store.wait()
    for part in s_q + [sums, dx_out]:
        part.drain()


def step(x, dy, counts, masks, weights):
    scratch = [pltpu.VMEM(*spec) for spec in (LAYER_BUFFERS | COMM_BUFFERS).values()]
    scratch += [pltpu.SemaphoreType.DMA(shape) for shape in SEMS.values()]
    scratch += [pltpu.SemaphoreType.REGULAR] * 2
    return pl.pallas_call(
        step_kernel,
        out_shape=(
            jax.ShapeDtypeStruct(TOKENS, bf),
            jax.ShapeDtypeStruct(TOKENS, bf),
            jax.ShapeDtypeStruct((VROWS, WINDOW), f32),
            jax.ShapeDtypeStruct((CHUNKS, 2, 384, 128), bf),
            jax.ShapeDtypeStruct((CHUNKS, 2, 48, WIDE), bf),
            jax.ShapeDtypeStruct((2, 48, D), bf),
            jax.ShapeDtypeStruct((3, 2, 48, D), bf),
        ),
        in_specs=[ANY, ANY, SMEM, SMEM] + [ANY] * 5,
        out_specs=[ANY] * 7,
        scratch_shapes=scratch,
        compiler_params=pltpu.CompilerParams(
            collective_id=1, has_side_effects=True, vmem_limit_bytes=63 * MIB + 512 * 1024
        ),
    )(x, dy, counts, masks, *weights)


def update_kernel(*refs):
    states = [refs[5 * n : 5 * n + 5] for n in range(3)]
    gv, *grads_in, y_in, dx_in = refs[15:22]
    y, dx = refs[22:24]
    news = [refs[24 + 5 * n : 29 + 5 * n] for n in range(3)]
    b_qkv, b_o, b_up, b_dn, b_vec, g_dn, g_up, g_o, g_q, g_vec = refs[39:49]
    out, low, wide, s_in, s_out, s_grad, s_tok, s_vec = refs[49:]
    boxes = (b_qkv, b_o, b_up, b_dn)
    load_y = pltpu.make_async_copy(y_in, out, s_tok.at[0])
    load_dx = pltpu.make_async_copy(dx_in, low, s_tok.at[1])
    store_dx = pltpu.make_async_copy(wide, dx, s_tok.at[2])
    store_y = pltpu.make_async_copy(out, y, s_tok.at[3])
    grad_loads = [
        pltpu.make_async_copy(src, dst, s_grad.at[n])
        for n, (src, dst) in enumerate(zip(grads_in, (g_dn, g_up, g_o, g_q)))
    ]
    vec_loads = [pltpu.make_async_copy(states[k][4], b_vec.at[k], s_vec.at[k]) for k in range(3)]
    vec_loads.append(pltpu.make_async_copy(gv, g_vec, s_vec.at[3]))
    vec_stores = [pltpu.make_async_copy(b_vec.at[k], news[k][4], s_vec.at[4 + k]) for k in range(3)]
    parts = [(1, pl.ds(0, 96))]
    parts += [(2, pl.ds(48 * h, 48)) for h in range(2)]
    parts += [(0, pl.ds(48 * h, 48)) for h in range(2)]
    parts += [(3, pl.ds(128 * c, 128)) for c in range(CHUNKS)]

    def load(n):
        a, rows = parts[n]
        return [
            pltpu.make_async_copy(states[k][a].at[rows], boxes[a].at[k, rows], s_in.at[n, k]) for k in range(3)
        ]

    def store(n):
        a, rows = parts[n]
        return [
            pltpu.make_async_copy(boxes[a].at[k, rows], news[k][a].at[rows], s_out.at[n, k]) for k in range(3)
        ]

    def start(copies):
        for copy in copies:
            copy.start()

    def wait(copies):
        for copy in copies:
            copy.wait()

    start([grad_loads[2]] + load(0) + [grad_loads[1]] + load(1) + load(2))
    start(vec_loads + [grad_loads[3], load_dx, load_y])

    def update(a, rows, cols, grad):
        box = boxes[a]
        new = adamw(
            box[0, rows, cols], box[1, rows, cols], box[2, rows, cols], grad.astype(f32), rates[a], decays[a]
        )
        for k in range(3):
            box[k, rows, cols] = new[k]

    for n, (a, rows) in enumerate(parts):
        if n + 3 < len(parts):
            if n + 3 == 5:
                start([grad_loads[0]])
            start(load(n + 3))
        if n in (0, 1, 3, 5):
            grad_loads[(2, 1, None, 3, None, 0)[n]].wait()
        wait(load(n))
        if a == 1:
            for h in range(2):
                update(1, slice(48 * h, 48 * h + 48), slice(0, D), g_o[h])
        elif a == 2:
            h = n - 1
            for c in range(CHUNKS):
                for i in range(OWNERS):
                    cols = slice((3 * i + c) * 128, (3 * i + c + 1) * 128)
                    update(2, slice(48 * h, 48 * h + 48), cols, g_up[c, h, :, i * 128 : (i + 1) * 128])
        elif a == 0:
            h = n - 3
            for hq in range(3):
                for w in range(3):
                    cols = slice(w * D + hq * 256, w * D + hq * 256 + 256)
                    update(0, slice(48 * h, 48 * h + 48), cols, g_q[hq, h, :, w * 256 : w * 256 + 256])
        else:
            c = n - 5
            for h in range(2):
                update(
                    3,
                    slice(128 * c, 128 * c + 128),
                    slice(384 * h, 384 * h + 384),
                    g_dn[c, h].astype(f32).T,
                )
        start(store(n))
        if n == 2:
            load_dx.wait()
            wide[...] = low[...].astype(f32)
            load_y.wait()
            start([store_dx, store_y])
        if n == 4:
            wait(vec_loads)
            here = lax.axis_index("items")
            first = here * 96 - window_start(here)
            r_at = lax.broadcasted_iota(jnp.int32, (WINDOW, 96), 0)
            c_at = lax.broadcasted_iota(jnp.int32, (WINDOW, 96), 1)
            chosen = jnp.where(r_at - first == c_at, 1.0, 0.0)
            grad = jnp.dot(g_vec[...], chosen, preferred_element_type=f32, precision=lax.Precision.HIGHEST)
            new = adamw(b_vec[0], b_vec[1], b_vec[2], grad[:12], rates[4], decays[4])
            for k in range(3):
                b_vec[k] = new[k]
            start(vec_stores)

    for n in range(len(parts)):
        wait(store(n))
    wait([store_dx, store_y] + vec_stores)


def update(masters, firsts, seconds, gv, grads, y, dx):
    shapes = [jax.ShapeDtypeStruct(m.shape, f32) for m in masters]
    out = pl.pallas_call(
        update_kernel,
        out_shape=[jax.ShapeDtypeStruct(TOKENS, bf), jax.ShapeDtypeStruct(TOKENS, f32)] + shapes * 3,
        in_specs=[ANY] * 22,
        out_specs=[ANY] * 17,
        scratch_shapes=[
            pltpu.VMEM((3, 96, 3 * D), f32),
            pltpu.VMEM((3, 96, D), f32),
            pltpu.VMEM((3, 96, FF), f32),
            pltpu.VMEM((3, 384, D), f32),
            pltpu.VMEM((3, 12, 96), f32),
        ]
        + [pltpu.VMEM(g.shape, g.dtype) for g in (*grads, gv)]
        + [
            pltpu.VMEM(TOKENS, bf),
            pltpu.VMEM(TOKENS, bf),
            pltpu.VMEM(TOKENS, f32),
            pltpu.SemaphoreType.DMA((8, 3)),
            pltpu.SemaphoreType.DMA((8, 3)),
            pltpu.SemaphoreType.DMA((4,)),
            pltpu.SemaphoreType.DMA((4,)),
            pltpu.SemaphoreType.DMA((7,)),
        ],
        compiler_params=pltpu.CompilerParams(vmem_limit_bytes=63 * MIB),
    )(*masters, *firsts, *seconds, gv, *grads, y, dx)
    return out[0], out[1], [out[2 + 5 * k : 7 + 5 * k] for k in range(3)]


def plain_kernel(*refs):
    (xs, dys, counts, masks, w_qkv, w_o, w_up, w_dn, vecs, y, dx, gv, o_dn, o_up, o_o, o_q) = refs[:16]
    r = collections.namedtuple("Refs", list(LAYER_BUFFERS) + ["sem"])(*refs[16:])
    layer = Layer(r, Masks(counts, masks))
    loads = [(xs, r.x), (dys, r.dy), (w_qkv, r.wqkv), (w_o, r.wo), (w_up, r.wup), (w_dn, r.wdn), (vecs, r.vec)]

    def move(pairs):
        copies = [pltpu.make_async_copy(s, d, r.sem.at[n]) for n, (s, d) in enumerate(pairs)]
        for copy in copies:
            copy.start()
        for copy in copies:
            copy.wait()

    move(loads)
    layer.start()
    layer.spread_biases()
    for t in range(2):
        layer.norm_item(t)

    def part(n, _):
        layer.attend(n, {})
        return 0

    lax.fori_loop(0, 6, part, 0)
    layer.middle({})
    layer.feed({})
    move([(r.wup, o_up), (r.gdn, o_dn)])
    layer.turn(lambda k: k, lambda k, g: None, {})
    layer.out_grads()
    layer.attend_back({}, lambda k: k, lambda k, t: None)
    move(
        [(r.dy, y), (r.x, dx), (r.gv, gv), (r.wo, o_o)]
        + [(layer.qkv_grad(hq), o_q.at[hq]) for hq in range(3)]
    )


def plain_step(x, dy, counts, masks, weights):
    def swap(values):
        return lax.all_to_all(values, "blk", 0, 0, tiled=True)

    full = [lax.all_gather(w.astype(bf), "items", axis=0, tiled=True) for w in weights[:4]]
    vecs = lax.all_gather(weights[4].astype(bf), "items", axis=1, tiled=True).astype(f32)
    w_qkv = full[0].reshape(D, 3, 3, 256).transpose(2, 0, 1, 3).reshape(3, 4, 2, 2, 48, D)
    w_o = full[1].reshape(4, 2, 2, 48, D)
    w_up = full[2].reshape(D, OWNERS, CHUNKS, 128).transpose(2, 0, 1, 3).reshape(CHUNKS, 4, 2, 2, 48, WIDE)
    w_dn = full[3].reshape(OWNERS, CHUNKS, 128, D).transpose(1, 0, 2, 3).reshape(CHUNKS, 4, 2, 2, 64, D)
    vecs = jnp.pad(vecs, ((0, VROWS - vecs.shape[0]), (0, 0)))
    y, dx, gv, g_dn, g_up, g_o, g_q = pl.pallas_call(
        plain_kernel,
        out_shape=(
            jax.ShapeDtypeStruct(TOKENS, bf),
            jax.ShapeDtypeStruct(TOKENS, bf),
            jax.ShapeDtypeStruct((VROWS, D), f32),
            jax.ShapeDtypeStruct((CHUNKS, 4, 2, 2, 384, 128), bf),
            jax.ShapeDtypeStruct((CHUNKS, 4, 2, 2, 48, WIDE), bf),
            jax.ShapeDtypeStruct((4, 2, 2, 48, D), bf),
            jax.ShapeDtypeStruct((3, 4, 2, 2, 48, D), bf),
        ),
        in_specs=[ANY, ANY, SMEM, SMEM] + [ANY] * 5,
        out_specs=[ANY] * 7,
        scratch_shapes=[pltpu.VMEM(*spec) for spec in LAYER_BUFFERS.values()]
        + [pltpu.SemaphoreType.DMA((8,))],
        compiler_params=pltpu.CompilerParams(vmem_limit_bytes=63 * MIB),
    )(swap(x), swap(dy), counts, masks, w_qkv, w_o, w_up, w_dn, vecs)
    g_up = g_up.reshape(CHUNKS, D, OWNERS, 128).transpose(1, 2, 0, 3).reshape(D, FF)
    g_dn = g_dn.reshape(CHUNKS, OWNERS, D, 128).transpose(1, 0, 3, 2).reshape(FF, D)
    g_q = g_q.reshape(3, D, 3, 256).transpose(1, 2, 0, 3).reshape(D, 3 * D)

    def total(values, axis):
        share = lax.psum_scatter(values.astype(f32), "items", scatter_dimension=axis, tiled=True)
        return lax.psum(share, "blk")

    grads = [total(v, 0) for v in (g_q, g_o.reshape(D, D), g_up, g_dn)] + [total(gv[:12], 1)]
    return swap(y), swap(dx).astype(f32), grads


def body(block_input, block_cotangent, task_counts, group_mask, *states):
    masters, firsts, seconds = states[:5], states[5:10], states[10:]
    x = block_input.reshape(TOKENS)
    dy = block_cotangent.reshape(TOKENS)
    allowed = group_mask.transpose(1, 2, 0)
    if lax.axis_size("items") == OWNERS and lax.axis_size("blk") == GROUPS:
        y, dx, gv, *grads = step(x, dy, task_counts, allowed, masters)
        y, dx, new = update(masters, firsts, seconds, gv, grads, y, dx)
    else:
        y, dx, grads = plain_step(x, dy, task_counts, allowed, masters)
        parts = [
            adamw(masters[n], firsts[n], seconds[n], grads[n], rates[n], decays[n]) for n in range(5)
        ]
        new = [[part[k] for part in parts] for k in range(3)]
    return (y.reshape(block_input.shape), dx.reshape(block_input.shape), *new[0], *new[1], *new[2])


def solution(mesh):
    tokens = P("items", "blk", None, None)
    rows = P("items", None)
    state = (rows, rows, rows, rows, P(None, "items"))
    return jax.shard_map(
        body,
        mesh=mesh,
        in_specs=(tokens, tokens, P("items"), P("items", None, None)) + state * 3,
        out_specs=(tokens, tokens) + state * 3,
        check_vma=False,
    )
```

```python
import collections

import jax
import jax.numpy as jnp
from jax import lax
from jax.experimental import pallas as pl
from jax.experimental.pallas import tpu as pltpu
from jax.sharding import PartitionSpec as P

D = 768
H = 12
HD = 64
FF = 3072
GROUPS = 4
GROUP = 128
STEP = 5
CHUNKS = 3
WIDE = 1024
VROWS = 16
OWNERS = 8
MIB = 1024 * 1024

norm_eps = 1e-06
beta_one = 0.9
beta_two = 0.5
adam_eps = 1e-08
weight_decay = 0.1
rates = (0.1, 0.8, 0.1, 0.06, 1.0)
decays = (weight_decay, weight_decay, weight_decay, weight_decay, 0.0)
masked_value = -1e30

bf = jnp.bfloat16
f32 = jnp.float32
MESH = pl.DeviceIdType.MESH
ANY = pl.BlockSpec(memory_space=pl.ANY)
SMEM = pl.BlockSpec(memory_space=pltpu.SMEM)
TOKENS = (GROUPS, 2, GROUP, D)


def adamw(weight, first, second, grad, rate, decay_rate):
    first_new = beta_one * first + (1.0 - beta_one) * grad
    second_new = beta_two * second + (1.0 - beta_two) * grad * grad
    first_hat = first_new * (1.0 / (1.0 - beta_one**STEP))
    second_hat = second_new * (1.0 / (1.0 - beta_two**STEP))
    weight_new = weight - rate * (
        first_hat / (jnp.sqrt(second_hat) + adam_eps) + decay_rate * weight
    )
    return (weight_new, first_new, second_new)


def nn(a, b):
    return jnp.dot(a, b, preferred_element_type=f32)


def nt(a, b):
    return lax.dot_general(a, b, (((1,), (1,)), ((), ())), preferred_element_type=f32)


def tn(a, b):
    return lax.dot_general(a, b, (((0,), (0,)), ((), ())), preferred_element_type=f32)


def normal(values):
    mean = jnp.mean(values, -1, keepdims=True)
    centred = values - mean
    scale = lax.rsqrt(jnp.mean(centred * centred, -1, keepdims=True) + norm_eps)
    return centred * scale, scale


def norm_back(grad, normed, scale, gain):
    e = grad * gain
    along = jnp.mean(e * normed, -1, keepdims=True)
    return scale * (e - jnp.mean(e, -1, keepdims=True) - normed * along)


def rows_of(ref, g):
    block = ref[g]
    return block.reshape(2 * GROUP, block.shape[-1])


def halves(ref, k):
    block = ref[2 * k : 2 * k + 2]
    return block.reshape(512, block.shape[-1])


def put_rows(ref, g, values):
    ref[g] = values.reshape(2, GROUP, values.shape[-1])


def span256(g):
    return pl.ds(pl.multiple_of(g * 256, 256), 256)


def col_sum(values):
    return jnp.sum(values, 0, keepdims=True)


def stacked(pair, low):
    zero = jnp.zeros_like(pair)
    return jnp.concatenate([jnp.where(low, pair, zero), jnp.where(low, zero, pair)], 0)


def run_hooks(hooks, index, *digits, base=10):
    for at, hook in hooks.items():
        if not digits or at % base in digits:
            pl.when(index == at)(hook)


def up_block(c, i):
    lane = 3 * (i % 2) + c
    return slice(8 + i // 2, 9 + i // 2), slice(lane * 128, (lane + 1) * 128)


LAYER_BUFFERS = dict(
    x=(TOKENS, bf),
    dy=(TOKENS, bf),
    qkv=(TOKENS[:3] + (3 * D,), bf),
    o=(TOKENS, bf),
    x2=(TOKENS, f32),
    a2=(TOKENS, bf),
    a2t=((D, 1024), bf),
    dyt=((D, 1024), bf),
    gl=((1024, WIDE), bf),
    du=((1024, WIDE), bf),
    yacc=(TOKENS, f32),
    da2=(TOKENS, f32),
    dkv=((2, GROUPS * GROUP, 128), f32),
    eye=((256, 256), bf),
    stats=((H, GROUPS, 256), f32),
    vec=((VROWS, D), f32),
    bu=((CHUNKS, 1, WIDE), f32),
    gbu=((CHUNKS, 1, WIDE), f32),
    bqkv=((3, 1, D), f32),
    gv=((VROWS, D), f32),
    wqkv=((3, 4, 2, 2, 48, D), bf),
    wo=((4, 2, 2, 48, D), bf),
    wup=((CHUNKS, 4, 2, 2, 48, WIDE), bf),
    wdn=((CHUNKS, 4, 2, 2, 64, D), bf),
    gdn=((CHUNKS, 4, 2, 2, 384, 128), bf),
)


class Masks:
    def __init__(self, counts, masks):
        self.counts, self.masks, self.first = counts, masks, lax.axis_index("blk") * 2
        self.place = lax.broadcasted_iota(jnp.int32, (GROUP, 256), 0)

    def __call__(self, s, t, g):
        item = self.first + t
        open_first = self.masks[g, 0, item] * self.counts[item]
        parts = [jnp.where(self.place < open_first, s[:GROUP], masked_value)]
        for k in range(1, g + 1):
            part = s[k * GROUP : (k + 1) * GROUP]
            if k < g:
                part = part + (self.masks[g, k, item] - 1).astype(f32) * -masked_value
            parts.append(part)
        return jnp.concatenate(parts, 0)


class Layer:
    def __init__(self, refs, masks):
        self.r, self.masks = refs, masks
        self.low = lax.broadcasted_iota(jnp.int32, (1, 2 * HD), 1) < HD
        self.upper = lax.broadcasted_iota(jnp.int32, (2 * HD, 1), 0) < HD

    def start(self):
        r = self.r
        row = lax.broadcasted_iota(jnp.int32, (256, 256), 0)
        col = lax.broadcasted_iota(jnp.int32, (256, 256), 1)
        r.eye[...] = jnp.where(row == col, 1.0, 0.0).astype(bf)
        r.gv[...] = jnp.zeros_like(r.gv)
        r.gbu[...] = jnp.zeros_like(r.gbu)

    def turned(self, values):
        n = values.shape[1]
        return nt(self.r.eye[:n, :n], values).astype(bf)

    def turn_rows(self, ref, g, values):
        for m in range(3):
            ref[m * 256 : (m + 1) * 256, span256(g)] = self.turned(values[:, m * 256 : (m + 1) * 256])

    def own_heads(self, pair):
        return self.turned(jnp.where(self.upper, pair[:, :GROUP], pair[:, GROUP:]).astype(bf)).astype(bf)

    def qkv_grad(self, hq):
        return self.r.wdn.at[hq, :, :, :, pl.ds(0, 48), :]

    def vec(self, k):
        return self.r.vec[k : k + 1, :]

    def spread_biases(self):
        r = self.r
        for hq in range(3):
            for w, k in ((0, 4), (2, 5)):
                r.bqkv[hq, :, w * 256 : w * 256 + 256] = r.vec[k : k + 1, hq * 256 : hq * 256 + 256]
            r.bqkv[hq, :, 256:512] = jnp.zeros((1, 256), f32)
        for c in range(CHUNKS):
            for i in range(OWNERS):
                r.bu[c, :, i * 128 : (i + 1) * 128] = r.vec[up_block(c, i)]

    def first_norm(self, g):
        normed, _ = normal(rows_of(self.r.x, g).astype(f32))
        return (normed * self.vec(0) + self.vec(1)).astype(bf)

    def norm_item(self, t):
        r = self.r

        def step(g, _):
            normed, _ = normal(r.x[g, t].astype(f32))
            r.a2[g, t] = (normed * self.vec(0) + self.vec(1)).astype(bf)
            return 0

        lax.fori_loop(0, GROUPS, step, 0)

    def lanes(self, hq, hp, w):
        return pl.ds(pl.multiple_of(hq * D + w * 256 + hp * 128, 128), 128)

    def attend(self, part, hooks):
        r, low = self.r, self.low
        t, hq = part // 3, part % 3
        a1 = r.a2[:, t].reshape(GROUPS * GROUP, D)
        p = nn(a1, r.wqkv[hq].reshape(D, D)) + self.qkv_bias(hq)
        r.qkv[:, t, :, pl.ds(pl.multiple_of(hq * D, 128), D)] = p.astype(bf).reshape(GROUPS, GROUP, D)
        run_hooks(hooks, 3 * part, 0, base=3)

        def step(hp, _):
            lanes = [self.lanes(hq, hp, w) for w in range(3)]
            out = pl.ds(pl.multiple_of(hq * 256 + hp * 128, 128), 128)
            k2 = r.qkv[:, t, :, lanes[1]].reshape(GROUPS * GROUP, 128)
            v2 = self.turned(r.qkv[:, t, :, lanes[2]].reshape(GROUPS * GROUP, 128))
            for g in range(GROUPS):
                n = (g + 1) * GROUP
                qs = stacked(r.qkv[g, t, :, lanes[0]] * jnp.asarray(0.125, bf), low)
                s = self.masks(nt(k2[:n], qs), t, g)
                top = jnp.max(s, 0, keepdims=True)
                e = jnp.exp(s - top)
                total = jnp.sum(e, 0, keepdims=True)
                p = (e * (1.0 / total)).astype(bf)
                r.stats[6 * t + 2 * hq + hp, g : g + 1, :] = top + jnp.log(total)
                r.o[g, t, :, out] = self.own_heads(nn(v2[:, :n], p))
            run_hooks(hooks, 3 * part + 1 + hp, 1, 2, base=3)
            return 0

        lax.fori_loop(0, 2, step, 0)

    def qkv_bias(self, hq):
        return self.r.bqkv[hq]

    def middle(self, hooks):
        r = self.r

        def step(g, _):
            v = rows_of(r.x, g).astype(f32) + nn(rows_of(r.o, g), r.wo[...].reshape(D, D)) + self.vec(6)
            put_rows(r.x2, g, v)
            put_rows(r.yacc, g, v + self.vec(7))
            normed, _ = normal(v)
            a = (normed * self.vec(2) + self.vec(3)).astype(bf)
            put_rows(r.a2, g, a)
            self.turn_rows(r.a2t, g, a)
            dy = rows_of(r.dy, g)
            self.turn_rows(r.dyt, g, dy)
            put_rows(r.da2, g, jnp.zeros((256, D), f32))
            r.gv[7:8, :] += col_sum(dy.astype(f32))
            run_hooks(hooks, g)
            return 0

        lax.fori_loop(0, GROUPS, step, 0)

    def feed(self, hooks):
        r = self.r

        def column(c, j):
            cols = span256(j)
            wup = r.wup[c, :, :, :, :, cols].reshape(D, 256)
            wdn = r.wdn[c, j].reshape(256, D)
            for k in range(2):
                rows = slice(512 * k, 512 * k + 512)
                u = nn(halves(r.a2, k), wup) + r.bu[c, :, cols]
                u2 = u * u
                half = 0.5 * jnp.tanh(u * (0.7978845608028654 + 0.035677408136300125 * u2)) + 0.5
                r.gl[rows, cols] = (u * half).astype(bf)
                slope = half + u * (2.0 * half * (1.0 - half)) * (
                    0.7978845608028654 + 0.10703222440890037 * u2
                )
                d = (nt(halves(r.dy, k), wdn) * slope).astype(bf)
                r.du[rows, cols] = d
                r.gbu[c, :, cols] += col_sum(d.astype(f32))

        def chunk(c, _):
            def step(j, _):
                column(c, j)
                run_hooks(hooks, 10 * c + j, 0, 1, 2, 3)
                return 0

            def down_grad(h, _):
                down = nn(r.dyt[pl.ds(pl.multiple_of(h * 384, 384), 384), :], r.gl[...]).astype(bf)
                for i in range(OWNERS):
                    r.gdn[c, i // 2, i % 2, h] = down[:, i * 128 : (i + 1) * 128]
                return 0

            def up_back(k, _):
                rows = pl.ds(pl.multiple_of(512 * k, 512), 512)
                back = nt(r.du[rows, :], r.wup[c].reshape(D, WIDE))
                r.da2[pl.ds(2 * k, 2)] += back.reshape(2, 2, GROUP, D)
                return 0

            def up_grad(h, _):
                up = nn(r.a2t[pl.ds(pl.multiple_of(h * 384, 384), 384), :], r.du[...]).astype(bf)
                r.wup[c, pl.ds(2 * h, 2)] = up.reshape(2, 2, 2, 48, WIDE)
                return 0

            def down(k, _):
                rows = pl.ds(pl.multiple_of(512 * k, 512), 512)
                out = nn(r.gl[rows, :], r.wdn[c].reshape(WIDE, D))
                r.yacc[pl.ds(2 * k, 2)] += out.reshape(2, 2, GROUP, D)
                return 0

            lax.fori_loop(0, 4, step, 0)
            for n, act in enumerate((down_grad, up_back, up_grad, down)):
                lax.fori_loop(0, 2, act, 0)
                run_hooks(hooks, 10 * c + 4 + n, 4 + n)
            return 0

        lax.fori_loop(0, CHUNKS, chunk, 0)
        for c in range(CHUNKS):
            for i in range(OWNERS):
                r.gv[up_block(c, i)] = r.gbu[c, :, i * 128 : (i + 1) * 128]

    def turn(self, order, send, hooks):
        r = self.r

        def step(k, _):
            g = order(k)
            c = rows_of(r.da2, g)
            normed, scale = normal(rows_of(r.x2, g))
            r.gv[2:3, :] += col_sum(c * normed)
            r.gv[3:4, :] += col_sum(c)
            d = rows_of(r.dy, g).astype(f32) + norm_back(c, normed, scale, self.vec(2))
            put_rows(r.dy, g, rows_of(r.yacc, g).astype(bf))
            send(k, g)
            put_rows(r.da2, g, d)
            r.gv[6:7, :] += col_sum(d)
            dz = d.astype(bf)
            put_rows(r.a2, g, dz)
            self.turn_rows(r.gl, g, rows_of(r.o, g))
            self.turn_rows(r.du, g, self.first_norm(g))
            put_rows(r.yacc, g, jnp.zeros((256, D), f32))
            run_hooks(hooks, k)
            return 0

        lax.fori_loop(0, GROUPS, step, 0)

    def out_grads(self):
        r = self.r

        def back(k, _):
            rows = pl.ds(2 * k, 2)
            do = nt(r.a2[rows].reshape(512, D), r.wo[...].reshape(D, D)).astype(bf)
            r.o[rows] = do.reshape(2, 2, GROUP, D)
            return 0

        def grad(h, _):
            part = r.gl[pl.ds(pl.multiple_of(h * 384, 384), 384), :]
            grads = nn(part, r.a2[...].reshape(GROUPS * 256, D)).astype(bf)
            r.wo[pl.ds(2 * h, 2)] = grads.reshape(2, 2, 2, 48, D)
            return 0

        lax.fori_loop(0, 2, back, 0)
        lax.fori_loop(0, 2, grad, 0)

    def attend_back(self, hooks, order, send):
        r, low = self.r, self.low

        def pair(hq, t, hp):
            lanes = [self.lanes(hq, hp, w) for w in range(3)]
            out = pl.ds(pl.multiple_of(hq * 256 + hp * 128, 128), 128)
            r.dkv[...] = jnp.zeros_like(r.dkv)
            k2 = r.qkv[:, t, :, lanes[1]].reshape(GROUPS * GROUP, 128)
            v2 = r.qkv[:, t, :, lanes[2]].reshape(GROUPS * GROUP, 128)
            turned_k = self.turned(k2)
            for g in range(GROUPS):
                n = (g + 1) * GROUP
                qs = stacked(r.qkv[g, t, :, lanes[0]] * jnp.asarray(0.125, bf), low)
                dos = stacked(r.o[g, t, :, out], low)
                s = self.masks(nt(k2[:n], qs), t, g)
                p = jnp.exp(s - r.stats[6 * t + 2 * hq + hp, g : g + 1, :])
                dp = nt(v2[:n], dos)
                ds = (p * (dp - jnp.sum(p * dp, 0, keepdims=True))).astype(bf)
                r.dkv[0, :n, :] += nn(ds, qs)
                r.dkv[1, :n, :] += nn(p.astype(bf), dos)
                r.qkv[g, t, :, lanes[0]] = self.own_heads(nn(turned_k[:, :n], ds) * 0.125)
            for w in range(2):
                r.qkv[:, t, :, lanes[w + 1]] = r.dkv[w].astype(bf).reshape(GROUPS, GROUP, 128)

        def quad(hq, _):
            cols = pl.ds(pl.multiple_of(hq * D, 128), D)

            def item(t, _):
                def step(hp, _):
                    pair(hq, t, hp)
                    run_hooks(hooks, 10 * hq + 2 * t + hp, 0, 1, 2, 3)
                    return 0

                lax.fori_loop(0, 2, step, 0)
                pl.when(t == 1)(lambda: grads(hq, cols))
                run_hooks(hooks, 10 * hq + 4 + t, 4, 5)
                rows = r.qkv[:, t, :, cols].reshape(512, D)
                back = nt(rows, r.wqkv[hq].reshape(D, D))
                r.yacc[:, t] += back.reshape(GROUPS, GROUP, D)
                run_hooks(hooks, 10 * hq + 6 + t, 6, 7)

                @pl.when(hq == 2)
                def _():
                    lax.fori_loop(0, GROUPS, lambda k, _: finish(t, k), 0)
                    run_hooks(hooks, 10 * hq + 8 + t, 8, 9)

                return 0

            lax.fori_loop(0, 2, item, 0)
            return 0

        def grads(hq, cols):
            d = r.qkv[:, :, :, cols].reshape(GROUPS * 256, D)

            def grad(h, _):
                part = r.du[pl.ds(pl.multiple_of(h * 384, 384), 384), :]
                out = nn(part, d).astype(bf)
                r.wdn[hq, pl.ds(2 * h, 2), :, :, :48, :] = out.reshape(2, 2, 2, 48, D)
                return 0

            lax.fori_loop(0, 2, grad, 0)
            sums = col_sum(d.astype(f32))
            r.gv[4:5, span256(hq)] = sums[:, :256]
            r.gv[5:6, span256(hq)] = sums[:, 512:]

        def finish(t, k):
            g = order(k)
            c = r.yacc[g, t]
            normed, scale = normal(r.x[g, t].astype(f32))
            r.gv[0:1, :] += col_sum(c * normed)
            r.gv[1:2, :] += col_sum(c)
            d = r.da2[g, t] + norm_back(c, normed, scale, self.vec(0))
            r.x[g, t] = d.astype(bf)
            send(k, t)
            return 0

        lax.fori_loop(0, 3, quad, 0)


class Here:
    def __init__(self):
        self.i, self.b = lax.axis_index("items"), lax.axis_index("blk")
        self.z, self.y = self.i // 2, self.i % 2
        self.x, self.c = self.b // 2, self.b % 2

    def z_plus(self, k):
        return (self.z + k) % 4

    def at_z(self, k):
        return (2 * self.z_plus(k) + self.y, self.b)

    def at_y(self):
        return (self.i + 1 - 2 * self.y, self.b)

    def at_x(self):
        return (self.i, (self.b + 2) % 4)

    def at_core(self):
        return (self.i, self.b + 1 - 2 * self.c)

    def at_blk(self, k):
        return (self.i, (self.b + k) % 4)

    def at_items(self, k):
        return ((self.i + k) % OWNERS, self.b)


def remote(src, dst, send, recv, device):
    return pltpu.make_async_remote_copy(
        src_ref=src, dst_ref=dst, send_sem=send, recv_sem=recv, device_id=device, device_id_type=MESH
    )


class Mail:
    def __init__(self, here, send, recv):
        self.here, self.send, self.recv = here, send, recv

    def go(self, src, dst, slot, device):
        remote(src, dst, self.send.at[slot], self.recv.at[slot], device).start()

    def arrived(self, dst, slot):
        remote(dst, dst, self.send.at[slot], self.recv.at[slot], self.here.at_core()).wait_recv()

    def left(self, src, *slots):
        for slot in slots:
            remote(src, src, self.send.at[slot], self.recv.at[slot], self.here.at_core()).wait_send()


class Gather(Mail):
    slots = 5

    def __init__(self, here, dst, send, recv):
        super().__init__(here, send, recv)
        self.dst = dst

    def first(self):
        h = self.here
        own = self.dst.at[h.z, h.y, h.c]
        for k in (1, 2, 3):
            self.go(own, own, k - 1, h.at_z(k))

    def second(self):
        h = self.here
        for k in (1, 2, 3):
            self.arrived(self.dst.at[h.z_plus(4 - k), h.y, h.c], k - 1)
        line = self.dst.at[:, h.y, h.c]
        self.go(line, line, 3, h.at_y())

    def third(self):
        h = self.here
        self.arrived(self.dst.at[:, 1 - h.y, h.c], 3)
        half = self.dst.at[:, :, h.c]
        self.go(half, half, 4, h.at_core())

    def last(self):
        self.arrived(self.dst.at[:, :, 1 - self.here.c], 4)

    def drain(self):
        self.left(self.dst.at[0, 0, 0], 0, 1, 2)
        self.left(self.dst.at[:, 0, 0], 3)
        self.left(self.dst.at[:, :, 0], 4)


class SplitGather(Gather):
    slots = 6

    def mine(self, z, y):
        h = self.here
        return self.dst.at[z, y, h.c, :, self.columns(h.x)]

    def columns(self, x):
        width = self.dst.shape[-1] // 2
        return pl.ds(pl.multiple_of(x * width, width), width)

    def first(self):
        h = self.here
        own = self.mine(h.z, h.y)
        for k in (1, 2, 3):
            self.go(own, own, k - 1, h.at_z(k))

    def second(self):
        h = self.here
        for k in (1, 2, 3):
            self.arrived(self.mine(h.z_plus(4 - k), h.y), k - 1)
        line = self.mine(slice(None), h.y)
        self.go(line, line, 3, h.at_y())

    def across(self):
        h = self.here
        self.arrived(self.mine(slice(None), 1 - h.y), 3)
        part = self.mine(slice(None), slice(None))
        self.go(part, part, 5, h.at_x())

    def third(self):
        h = self.here
        self.arrived(self.dst.at[:, :, h.c, :, self.columns(1 - h.x)], 5)
        half = self.dst.at[:, :, h.c]
        self.go(half, half, 4, h.at_core())

    def drain(self):
        self.left(self.mine(0, 0), 0, 1, 2)
        self.left(self.mine(slice(None), 0), 3)
        self.left(self.dst.at[:, :, 0], 4)
        self.left(self.mine(slice(None), slice(None)), 5)


class Exchange(Mail):
    def __init__(self, here, src, dst, send, recv, local):
        super().__init__(here, send, recv)
        self.src, self.dst, self.local = src, dst, local

    def own(self):
        h = self.here
        return pltpu.make_async_copy(self.src.at[h.b], self.dst.at[h.b], self.local)

    def order(self, k):
        h = self.here
        odd, near = k % 2, k // 2
        far = (1 - odd) * ((h.b + 2) % 4) + odd * (3 - h.b)
        return (1 - near) * far + near * (h.b + (1 - odd) * (1 - 2 * h.c))

    def copy(self, k):
        h = self.here
        to = self.order(k)
        return remote(self.src.at[to], self.dst.at[h.b], self.send.at[k], self.recv.at[k], (h.i, to))

    def put(self, k, _=None):
        @pl.when(k < 3)
        def _():
            self.copy(k).start()

        @pl.when(k == 3)
        def _():
            self.own().start()

    def start(self):
        for k in range(3):
            self.copy(k).start()
        self.own().start()

    def arrive(self):
        self.own().wait()
        for k in range(3):
            self.arrived(self.dst.at[self.order(k)], k)

    def drain(self):
        for k in range(3):
            self.copy(k).wait_send()


class ItemExchange(Exchange):
    def copy(self, k, t):
        h = self.here
        to, slot = self.order(k), 3 * t + k
        return remote(
            self.src.at[to, t], self.dst.at[h.b, t], self.send.at[slot], self.recv.at[slot], (h.i, to)
        )

    def own(self, t):
        h = self.here
        return pltpu.make_async_copy(self.src.at[h.b, t], self.dst.at[h.b, t], self.local.at[t])

    def put(self, k, t):
        @pl.when(k < 3)
        def _():
            self.copy(k, t).start()

        @pl.when(k == 3)
        def _():
            self.own(t).start()

    def start(self, t):
        for k in range(3):
            self.copy(k, t).start()
        self.own(t).start()

    def arrive(self, t):
        self.own(t).wait()
        for k in range(3):
            self.arrived(self.dst.at[self.order(k), t], 3 * t + k)

    def drain(self):
        self.left(self.src.at[0, 0], *range(6))


class Reduce(Mail):
    slots = 8

    def __init__(self, here, g, rc, place, count, credit, ry, rz, rx, total, out, send, recv):
        super().__init__(here, send, recv)
        self.g, self.rc, self.place, self.count, self.credit = g, rc, place, count, credit
        self.ry, self.rz, self.rx, self.total, self.out = ry, rz, rx, total, out

    def over_core(self):
        h = self.here
        if self.place is not None and self.place >= 2:
            pl.semaphore_wait(self.credit, 1)
        self.go(self.g.at[:, :, 1 - h.c], self.rc, 0, h.at_core())

    def over_y(self):
        h = self.here
        self.arrived(self.rc, 0)

        def add(n, _):
            z, y = n // 2, n % 2
            self.g[z, y, h.c] = self.g[z, y, h.c] + self.rc[z, y]
            return 0

        lax.fori_loop(0, 8, add, 0)
        if self.place is not None and self.place + 2 < self.count:
            pl.semaphore_signal(self.credit, inc=1, device_id=h.at_core(), device_id_type=MESH)
        self.go(self.g.at[:, 1 - h.y, h.c], self.ry, 1, h.at_y())

    def over_z(self):
        h = self.here
        self.arrived(self.ry, 1)

        def add(z, _):
            self.g[z, h.y, h.c] = self.g[z, h.y, h.c] + self.ry[z]
            return 0

        lax.fori_loop(0, 4, add, 0)
        for k in (2, 1, 3):
            self.go(self.g.at[h.z_plus(k), h.y, h.c], self.rz.at[k - 1], 1 + k, h.at_z(k))

    def over_x(self):
        h = self.here
        part = self.g[h.z, h.y, h.c].astype(f32)
        for k in (1, 2, 3):
            self.arrived(self.rz.at[k - 1], 1 + k)
            part = part + self.rz[k - 1].astype(f32)
        self.total[0] = part.astype(bf)
        self.go(self.total.at[0], self.rx, 5, h.at_x())

    def share(self):
        h = self.here
        self.arrived(self.rx, 5)
        self.total[1] = self.total[0] + self.rx[...]
        self.own().start()
        self.go(self.total.at[1], self.out.at[h.c], 6, h.at_core())

    def own(self):
        return pltpu.make_async_copy(self.total.at[1], self.out.at[self.here.c], self.send.at[7])

    def last(self):
        self.arrived(self.out.at[1 - self.here.c], 6)
        self.own().wait()

    def drain(self):
        self.left(self.rc, 0)
        self.left(self.ry, 1)
        self.left(self.rz.at[0], 2, 3, 4)
        self.left(self.rx, 5, 6)


class SplitReduce(Reduce):
    slots = 9

    def __init__(self, rx0, *args):
        super().__init__(*args)
        self.rx0 = rx0

    def rows(self, x):
        count = self.g.shape[-2] // 2
        return pl.ds(pl.multiple_of(x * count, count), count)

    def over_x0(self):
        h = self.here
        self.arrived(self.rc, 0)

        def add(n, _):
            z, y = n // 2, n % 2
            self.g[z, y, h.c] = self.g[z, y, h.c] + self.rc[z, y]
            return 0

        lax.fori_loop(0, 8, add, 0)
        if self.place + 2 < self.count:
            pl.semaphore_signal(self.credit, inc=1, device_id=h.at_core(), device_id_type=MESH)
        self.go(self.g.at[:, :, h.c, self.rows(1 - h.x)], self.rx0, 8, h.at_x())

    def over_y(self):
        h = self.here
        mine = self.rows(h.x)
        self.arrived(self.rx0, 8)

        def add(n, _):
            z, y = n // 2, n % 2
            self.g[z, y, h.c, mine] = self.g[z, y, h.c, mine] + self.rx0[z, y]
            return 0

        lax.fori_loop(0, 8, add, 0)
        self.go(self.g.at[:, 1 - h.y, h.c, mine], self.ry.at[:, self.rows(0)], 1, h.at_y())

    def over_z(self):
        h = self.here
        mine, box = self.rows(h.x), self.rows(0)
        self.arrived(self.ry.at[:, box], 1)

        def add(z, _):
            self.g[z, h.y, h.c, mine] = self.g[z, h.y, h.c, mine] + self.ry[z, box]
            return 0

        lax.fori_loop(0, 4, add, 0)
        for k in (2, 1, 3):
            self.go(self.g.at[h.z_plus(k), h.y, h.c, mine], self.rz.at[k - 1, box], 1 + k, h.at_z(k))

    def over_x(self):
        h = self.here
        mine, box = self.rows(h.x), self.rows(0)
        part = self.g[h.z, h.y, h.c, mine].astype(f32)
        for k in (1, 2, 3):
            self.arrived(self.rz.at[k - 1, box], 1 + k)
            part = part + self.rz[k - 1, box].astype(f32)
        self.total[1, mine] = part.astype(bf)
        done = self.total.at[1, mine]
        self.go(done, done, 5, h.at_x())

    def share(self):
        h = self.here
        self.arrived(self.total.at[1, self.rows(1 - h.x)], 5)
        self.own().start()
        self.go(self.total.at[1], self.out.at[h.c], 6, h.at_core())

    def drain(self):
        box = self.rows(0)
        self.left(self.rc, 0)
        self.left(self.ry.at[:, box], 1)
        self.left(self.rz.at[0, box], 2, 3, 4)
        self.left(self.total.at[1, box], 5)
        self.left(self.rx, 6)
        self.left(self.rx0, 8)


WINDOW = 256


def window_start(owner):
    return (3 * owner // 4 - owner // 7) * 128


def window_of(owner):
    return pl.ds(pl.multiple_of(window_start(owner), 128), WINDOW)


class ReduceVectors(Mail):
    def __init__(self, here, v, blk_inbox, items_inbox, out, send, recv):
        super().__init__(here, send, recv)
        self.v, self.blk_inbox, self.items_inbox, self.out = v, blk_inbox, items_inbox, out

    def first(self):
        h = self.here
        self.blk_inbox[h.b] = self.v[...]
        for k in (1, 2, 3):
            self.go(self.v, self.blk_inbox.at[h.b], k - 1, h.at_blk(k))

    def second(self):
        h = self.here
        for k in (1, 2, 3):
            self.arrived(self.blk_inbox.at[(h.b + 4 - k) % 4], k - 1)
        self.left(self.v, 0, 1, 2)
        box = self.blk_inbox
        self.v[...] = (box[0] + box[1]) + (box[2] + box[3])
        for k in range(1, OWNERS):
            owner = (h.i + k) % OWNERS
            self.go(
                self.v.at[:, window_of(owner)], self.items_inbox.at[h.i], 2 + k, h.at_items(k)
            )
        self.items_inbox[h.i] = self.v[:, window_of(h.i)]

    def third(self):
        h = self.here
        for k in range(1, OWNERS):
            self.arrived(self.items_inbox.at[(h.i + OWNERS - k) % OWNERS], 2 + k)
        total = self.items_inbox[0]
        for n in range(1, OWNERS):
            total = total + self.items_inbox[n]
        self.out[...] = total

    def drain(self):
        self.left(self.out, *range(3, 10))


INBOXES = (("d", CHUNKS, 384, 128), ("u", CHUNKS, 48, WIDE), ("q", 4, 48, D))
COMM_BUFFERS = dict(
    rcd=((2, 4, 2, 384, 128), bf),
    rcu=((2, 4, 2, 48, WIDE), bf),
    vbox=((OWNERS, VROWS, WINDOW), bf),
    gbox=((GROUPS, VROWS, D), f32),
    wbox=((OWNERS, VROWS, WINDOW), f32),
    gvw=((VROWS, WINDOW), f32),
    wvec=((12, 96), f32),
    rx0=((2, 4, 2, 192, 128), bf),
)
for _kind, _n, _rows, _cols in INBOXES:
    COMM_BUFFERS["ry" + _kind] = ((_n, 4, _rows, _cols), bf)
    COMM_BUFFERS["rz" + _kind] = ((_n, 3, _rows, _cols), bf)
    COMM_BUFFERS["rx" + _kind] = ((_n, _rows, _cols), bf)
    COMM_BUFFERS["tt" + _kind] = ((_n, 2, _rows, _cols), bf)
SEMS = dict(
    load=(12,),
    gsend=(12, SplitGather.slots),
    grecv=(12, SplitGather.slots),
    rsend=(12, SplitReduce.slots),
    rrecv=(12, SplitReduce.slots),
    xsend=(2, 6),
    xrecv=(2, 6),
    xlocal=(2, 2),
    esend=(2, 3),
    erecv=(2, 3),
    local=(5,),
    vsend=(7,),
    vrecv=(7,),
    wsend=(10,),
    wrecv=(10,),
)


SPLIT_DOWN = (1, 2)
MOVES = dict(
    a="first", l="second", xx="across", h="third", w="last",
    core="over_core", x0="over_x0", y="over_y", z="over_z", x="over_x", sh="share", end="last",
)
TIMETABLE = dict(
    start=(("Q0q", "a"), ("Q0k", "a"), ("Q0v", "a"),),
    table=(("Q0q", "l"), ("Q0k", "l"), ("Q1", "a"), ("Q0q", "h"), ("Q0v", "l"), ("Q2", "a"), ("Q0k", "h"), ("Q0q", "w"),),
    ln0=(("Q0v", "h"), ("Q0k", "w"), ("Q0v", "w"),),
    s0a=(("Q1", "l"), ("O", "a"),),
    s0b=(("Q2", "l"), ("U0", "a"), ("Q1", "h"), ("Q1", "w"),),
    s1p=(("O", "l"), ("D0", "a"),),
    s1b=(("Q2", "h"), ("U0", "l"), ("U1", "a"), ("Q2", "w"),),
    s2a=(("O", "h"),),
    s3a=(("O", "w"), ("U0", "xx"), ("D0", "l"), ("D1", "a"),),
    s4b=(("U1", "l"), ("U2", "a"),),
    m1=(("U0", "h"), ("D0", "h"),),
    m3=(("D1", "l"), ("D2", "a"), ("U0", "w"), ("U1", "xx"), ("D0", "w"),),
    f00=(("U2", "l"),),
    f03=(("D1", "h"),),
    g00=(("U1", "h"), ("d0", "core"),),
    g01=(("D1", "w"), ("U2", "xx"), ("D2", "l"),),
    g02=(("U1", "w"), ("u0", "core"),),
    f10=(("d0", "y"),),
    f11=(("u0", "y"),),
    f13=(("U2", "h"), ("D2", "h"),),
    g10=(("d1", "core"),),
    g11=(("U2", "w"),),
    g12=(("u1", "core"),),
    g13=(("D2", "w"), ("d0", "z"),),
    f20=(("d1", "x0"),),
    f21=(("u1", "y"),),
    g20=(("u0", "z"), ("d2", "core"),),
    g21=(("d0", "x"),),
    g22=(("d1", "y"), ("d2", "x0"), ("u2", "core"),),
    g23=(("d0", "sh"),),
    t1=(("u1", "z"), ("u2", "y"), ("d0", "end"),),
    t3=(("u0", "x"),),
    gwo=(("d1", "z"), ("o", "core"),),
    b00=(("d2", "y"),),
    b01=(("o", "y"),),
    b02=(("u1", "x"),),
    b03=(("u2", "z"),),
    gq0=(("d1", "x"), ("q0", "core"),),
    b10=(("d2", "z"),),
    b11=(("q0", "y"),),
    b13=(("o", "z"), ("u2", "x"),),
    gq1=(("q1", "core"),),
    on11=(("u0", "sh"),),
    b20=(("u1", "sh"), ("d2", "x"),),
    b21=(("u0", "end"), ("d1", "sh"), ("u1", "end"), ("q0", "z"), ("q1", "y"),),
    on20=(("u2", "sh"), ("d1", "end"),),
    fin0=(("d2", "sh"),),
    b22=(("u2", "end"), ("o", "x"), ("d2", "end"),),
    gq2=(("q2q", "core"), ("q2k", "core"), ("q2v", "core"),),
    on21=(("q1", "z"),),
    fin1=(("q2q", "y"), ("q2k", "y"), ("q0", "x"),),
    tail0=(("q2v", "y"), ("o", "sh"), ("q2q", "z"), ("o", "end"), ("q2k", "z"), ("q1", "x"), ("q2v", "z"), ("q2q", "x"), ("q2k", "x"), ("q0", "sh"), ("q2v", "x"),),
    tail1=(("q0", "end"), ("q1", "sh"), ("q2q", "sh"), ("q2k", "sh"), ("q2v", "sh"), ("q1", "end"), ("q2q", "end"),),
    tail2=(("q2k", "end"), ("q2v", "end"),),
)


def step_kernel(*refs):
    (xs, dys, counts, masks, w_qkv, w_o, w_up, w_dn, w_vec, y, dx, gv, o_dn, o_up, o_o, o_q) = refs[:16]
    names = list(LAYER_BUFFERS) + list(COMM_BUFFERS) + list(SEMS) + ["credit_d", "credit_u"]
    r = collections.namedtuple("Refs", names)(*refs[16:])
    here = Here()
    barrier = pltpu.get_barrier_semaphore()
    friends = [here.at_items(k) for k in range(1, OWNERS)] + [here.at_blk(k) for k in (1, 2, 3)]
    for device in friends:
        pl.semaphore_signal(barrier, inc=1, device_id=device, device_id_type=MESH)

    half = pl.ds(here.c * 48, 48)
    small, small_dn = pl.ds(0, 48), pl.ds(0, 64)
    loads = []
    for q in range(3):
        loads.append((w_qkv.at[half, pl.ds(q * D, D)], r.x2.at[q // 2, q % 2, small, :]))
    loads.append((w_o.at[half], r.x2.at[1, 1, small, :]))
    for q in range(4):
        loads.append((w_up.at[half, pl.ds(q * D, D)], r.x2.at[2 + q // 2, q % 2, small, :]))
    for q in range(3):
        rows = pl.ds(q * 128 + here.c * 64, 64)
        loads.append((w_dn.at[rows], r.yacc.at[q // 2, q % 2, small_dn, :]))
    loads.append((w_vec, r.wvec))
    loads = [pltpu.make_async_copy(s, d, r.load.at[n]) for n, (s, d) in enumerate(loads)]
    for load in loads:
        load.start()

    layer = Layer(r, Masks(counts, masks))
    pl.semaphore_wait(barrier, len(friends))

    x_in = ItemExchange(here, xs, r.x, r.xsend.at[0], r.xrecv.at[0], r.xlocal.at[0])
    dy_in = Exchange(here, dys, r.dy, r.esend.at[0], r.erecv.at[0], r.local.at[1])
    y_out = Exchange(here, r.dy, y, r.esend.at[1], r.erecv.at[1], r.local.at[2])
    dx_out = ItemExchange(here, r.x, dx, r.xsend.at[1], r.xrecv.at[1], r.xlocal.at[1])

    count = iter(range(12))

    def gather(dst, parts, kind=Gather):
        width = dst.shape[-1] // parts
        units = []
        for p in range(parts):
            n = next(count)
            part = dst.at[:, :, :, :, pl.ds(p * width, width)]
            units.append(kind(here, part, r.gsend.at[n], r.grecv.at[n]))
        return units

    g_q = [gather(r.wqkv.at[hq], 1 if hq else 3) for hq in range(3)]
    (g_o,) = gather(r.wo, 1)
    g_u = [gather(r.wup.at[c], 1, SplitGather) for c in range(CHUNKS)]
    g_d = [gather(r.wdn.at[c], 1) for c in range(CHUNKS)]

    def reduce(kind, n, index, g, rc, place, count, credit, out):
        boxes = [getattr(r, box + kind).at[n] for box in ("ry", "rz", "rx", "tt")]
        args = (here, g, rc, place, count, credit, *boxes, out, r.rsend.at[index], r.rrecv.at[index])
        if kind == "d" and n in SPLIT_DOWN:
            return SplitReduce(r.rx0.at[n - 1], *args)
        return Reduce(*args)

    s_d = [
        reduce("d", c, 2 * c, r.gdn.at[c], r.rcd.at[c % 2], c, 3, r.credit_d, o_dn.at[c])
        for c in range(CHUNKS)
    ]
    s_u = [
        reduce("u", c, 2 * c + 1, r.wup.at[c], r.rcu.at[c % 2], c, 7, r.credit_u, o_up.at[c])
        for c in range(CHUNKS)
    ]
    narrow = [r.rcu.at[n % 2, :, :, :, pl.ds(0, D)] for n in range(2)]
    s_o = reduce("q", 3, 6, r.wo, narrow[1], 3, 7, r.credit_u, o_o)
    s_q = [
        reduce("q", c, 7 + c, layer.qkv_grad(c), narrow[c % 2], 4 + c, 7, r.credit_u, o_q.at[c])
        for c in range(2)
    ]
    for w in range(3):
        third = pl.ds(256 * w, 256)
        boxes = [r.ryq.at[2, :, :, third], r.rzq.at[2, :, :, third], r.rxq.at[2, :, third], r.ttq.at[2, :, :, third]]
        s_q.append(
            Reduce(
                here, r.wdn.at[2, :, :, :, pl.ds(0, 48), third], r.rcu.at[0, :, :, :, third],
                6 if w == 0 else None, 7, r.credit_u, *boxes, o_q.at[2, :, :, third],
                r.rsend.at[9 + w], r.rrecv.at[9 + w],
            )
        )
    sums = ReduceVectors(here, r.gv, r.gbox, r.wbox, r.gvw, r.wsend, r.wrecv)

    units = {"O": g_o, "o": s_o, "q0": s_q[0], "q1": s_q[1]}
    for c in range(CHUNKS):
        units |= {f"d{c}": s_d[c], f"u{c}": s_u[c]}
        for base, parts in (("Q", g_q[c]), ("U", g_u[c]), ("D", g_d[c])):
            names = ("q", "k", "v") if len(parts) > 1 else ("",)
            units |= {f"{base}{c}{name}": part for name, part in zip(names, parts)}
    units |= {f"q2{name}": part for name, part in zip("qkv", s_q[2:])}

    def at(slot):
        for unit, name in TIMETABLE.get(slot, ()):
            getattr(units[unit], MOVES[name])()

    def slots(**names):
        return {
            index: (lambda slot=slot: at(slot)) for slot, index in names.items() if slot in TIMETABLE
        }

    x_in.start(0)
    for q in range(3):
        loads[q].wait()
        part = r.x2[q // 2, q % 2, :48, :].astype(bf)
        for hq in range(3):
            r.wqkv[hq, here.z, here.y, here.c, :, q * 256 : q * 256 + 256] = part[:, hq * 256 : hq * 256 + 256]
    at("start")
    at("more")

    rows = lax.broadcasted_iota(jnp.int32, (96, WINDOW), 0)
    cols = lax.broadcasted_iota(jnp.int32, (96, WINDOW), 1)
    chosen = jnp.where(cols - (here.i * 96 - window_start(here.i)) == rows, 1.0, 0.0).astype(bf)
    loads[11].wait()
    r.vbox[here.i] = jnp.concatenate(
        [nn(r.wvec[...].astype(bf), chosen), jnp.zeros((VROWS - 12, WINDOW), f32)], 0
    ).astype(bf)
    table = Mail(here, r.vsend, r.vrecv)
    for k in range(1, OWNERS):
        own = r.vbox.at[here.i]
        table.go(own, own, k - 1, here.at_items(k))
    layer.start()
    loads[3].wait()
    r.wo[here.z, here.y, here.c] = r.x2[1, 1, :48, :].astype(bf)
    for q in range(4):
        loads[4 + q].wait()
        part = r.x2[2 + q // 2, q % 2, :48, :].astype(bf)
        for m in range(6):
            i, c = (6 * q + m) // 3, (6 * q + m) % 3

            @pl.when(here.x == i // 4)
            def _(i=i, c=c, part=part[:, m * 128 : (m + 1) * 128]):
                r.wup[c, here.z, here.y, here.c, :, i * 128 : (i + 1) * 128] = part

    for c in range(CHUNKS):
        loads[8 + c].wait()
        r.wdn[c, here.z, here.y, here.c] = r.yacc[c // 2, c % 2, :64, :].astype(bf)

    at("cast")
    for k in range(1, OWNERS):
        table.arrived(r.vbox.at[(here.i + OWNERS - k) % OWNERS], k - 1)
    r.vec[...] = jnp.zeros_like(r.vec)
    for n in range(OWNERS):
        start = window_start(n)
        r.vec[:, start : start + WINDOW] += r.vbox[n].astype(f32)
    layer.spread_biases()
    at("table")
    x_in.arrive(0)
    x_in.start(1)
    layer.norm_item(0)
    at("ln0")

    def other_item():
        x_in.arrive(1)
        layer.norm_item(1)

    in_parts = slots(**{f"s{n}{'pab'[j]}": 3 * n + j for n in range(6) for j in range(3)})
    for index, extra in ((2, dy_in.start), (8, other_item)):

        def both(before=in_parts.get(index, lambda: None), extra=extra):
            before()
            extra()

        in_parts[index] = both

    def part(n, _):
        layer.attend(n, in_parts)
        return 0

    lax.fori_loop(0, 6, part, 0)
    dy_in.arrive()
    at("dy")
    layer.middle(slots(**{f"m{k}": k for k in range(GROUPS)}))
    in_feed = {f"f{c}{j}": 10 * c + j for c in range(CHUNKS) for j in range(4)}
    in_feed |= {f"g{c}{n}": 10 * c + 4 + n for c in range(CHUNKS) for n in range(4)}
    in_feed = slots(**in_feed)
    for c in range(CHUNKS):

        def overwrite(c=c, before=in_feed.get(10 * c + 5, lambda: None)):
            before()
            for part in g_u[c]:
                part.drain()

        in_feed[10 * c + 5] = overwrite
    layer.feed(in_feed)
    dy_in.drain()
    layer.turn(y_out.order, y_out.put, slots(**{f"t{k}": k for k in range(GROUPS)}))
    g_o.drain()
    for part in g_d[0] + g_d[1] + g_d[2]:
        part.drain()
    layer.out_grads()
    at("gwo")
    in_back = {f"b{q}{k}": 10 * q + k for q in range(3) for k in range(4)}
    in_back |= {f"gq{q}": 10 * q + 5 for q in range(3)}
    in_back |= {f"on{q}{t}": 10 * q + 6 + t for q in range(3) for t in range(2)}
    in_back |= {f"fin{t}": 28 + t for t in range(2)}
    layer.attend_back(slots(**in_back), dx_out.order, dx_out.put)
    sums.first()
    y_out.arrive()
    for part in g_q[0] + g_q[1] + g_q[2] + [x_in, y_out]:
        part.drain()
    table.left(r.vbox.at[0], *range(OWNERS - 1))
    at("tail0")
    sums.second()
    for part in s_d + s_u + [s_o]:
        part.drain()
    at("tail1")
    sums.third()
    store = pltpu.make_async_copy(r.gvw, gv, r.local.at[4])
    store.start()
    at("tail2")
    dx_out.arrive(0)
    dx_out.arrive(1)
    store.wait()
    for part in s_q + [sums, dx_out]:
        part.drain()


def step(x, dy, counts, masks, weights):
    scratch = [pltpu.VMEM(*spec) for spec in (LAYER_BUFFERS | COMM_BUFFERS).values()]
    scratch += [pltpu.SemaphoreType.DMA(shape) for shape in SEMS.values()]
    scratch += [pltpu.SemaphoreType.REGULAR] * 2
    return pl.pallas_call(
        step_kernel,
        out_shape=(
            jax.ShapeDtypeStruct(TOKENS, bf),
            jax.ShapeDtypeStruct(TOKENS, bf),
            jax.ShapeDtypeStruct((VROWS, WINDOW), f32),
            jax.ShapeDtypeStruct((CHUNKS, 2, 384, 128), bf),
            jax.ShapeDtypeStruct((CHUNKS, 2, 48, WIDE), bf),
            jax.ShapeDtypeStruct((2, 48, D), bf),
            jax.ShapeDtypeStruct((3, 2, 48, D), bf),
        ),
        in_specs=[ANY, ANY, SMEM, SMEM] + [ANY] * 5,
        out_specs=[ANY] * 7,
        scratch_shapes=scratch,
        compiler_params=pltpu.CompilerParams(
            collective_id=1, has_side_effects=True, vmem_limit_bytes=63 * MIB + 512 * 1024
        ),
    )(x, dy, counts, masks, *weights)


def update_kernel(*refs):
    states = [refs[5 * n : 5 * n + 5] for n in range(3)]
    gv, *grads_in, y_in, dx_in = refs[15:22]
    y, dx = refs[22:24]
    news = [refs[24 + 5 * n : 29 + 5 * n] for n in range(3)]
    b_qkv, b_o, b_up, b_dn, b_vec, g_dn, g_up, g_o, g_q, g_vec = refs[39:49]
    out, low, wide, s_in, s_out, s_grad, s_tok, s_vec = refs[49:]
    boxes = (b_qkv, b_o, b_up, b_dn)
    load_y = pltpu.make_async_copy(y_in, out, s_tok.at[0])
    load_dx = pltpu.make_async_copy(dx_in, low, s_tok.at[1])
    store_dx = pltpu.make_async_copy(wide, dx, s_tok.at[2])
    store_y = pltpu.make_async_copy(out, y, s_tok.at[3])
    grad_loads = [
        pltpu.make_async_copy(src, dst, s_grad.at[n])
        for n, (src, dst) in enumerate(zip(grads_in, (g_dn, g_up, g_o, g_q)))
    ]
    vec_loads = [pltpu.make_async_copy(states[k][4], b_vec.at[k], s_vec.at[k]) for k in range(3)]
    vec_loads.append(pltpu.make_async_copy(gv, g_vec, s_vec.at[3]))
    vec_stores = [pltpu.make_async_copy(b_vec.at[k], news[k][4], s_vec.at[4 + k]) for k in range(3)]
    parts = [(1, pl.ds(0, 96))]
    parts += [(2, pl.ds(48 * h, 48)) for h in range(2)]
    parts += [(0, pl.ds(48 * h, 48)) for h in range(2)]
    parts += [(3, pl.ds(128 * c, 128)) for c in range(CHUNKS)]

    def load(n):
        a, rows = parts[n]
        return [
            pltpu.make_async_copy(states[k][a].at[rows], boxes[a].at[k, rows], s_in.at[n, k]) for k in range(3)
        ]

    def store(n):
        a, rows = parts[n]
        return [
            pltpu.make_async_copy(boxes[a].at[k, rows], news[k][a].at[rows], s_out.at[n, k]) for k in range(3)
        ]

    def start(copies):
        for copy in copies:
            copy.start()

    def wait(copies):
        for copy in copies:
            copy.wait()

    start([grad_loads[2]] + load(0) + [grad_loads[1]] + load(1) + load(2))
    start(vec_loads + [grad_loads[3], load_dx, load_y])

    def update(a, rows, cols, grad):
        box = boxes[a]
        new = adamw(
            box[0, rows, cols], box[1, rows, cols], box[2, rows, cols], grad.astype(f32), rates[a], decays[a]
        )
        for k in range(3):
            box[k, rows, cols] = new[k]

    for n, (a, rows) in enumerate(parts):
        if n + 3 < len(parts):
            if n + 3 == 5:
                start([grad_loads[0]])
            start(load(n + 3))
        if n in (0, 1, 3, 5):
            grad_loads[(2, 1, None, 3, None, 0)[n]].wait()
        wait(load(n))
        if a == 1:
            for h in range(2):
                update(1, slice(48 * h, 48 * h + 48), slice(0, D), g_o[h])
        elif a == 2:
            h = n - 1
            for c in range(CHUNKS):
                for i in range(OWNERS):
                    cols = slice((3 * i + c) * 128, (3 * i + c + 1) * 128)
                    update(2, slice(48 * h, 48 * h + 48), cols, g_up[c, h, :, i * 128 : (i + 1) * 128])
        elif a == 0:
            h = n - 3
            for hq in range(3):
                for w in range(3):
                    cols = slice(w * D + hq * 256, w * D + hq * 256 + 256)
                    update(0, slice(48 * h, 48 * h + 48), cols, g_q[hq, h, :, w * 256 : w * 256 + 256])
        else:
            c = n - 5
            for h in range(2):
                update(
                    3,
                    slice(128 * c, 128 * c + 128),
                    slice(384 * h, 384 * h + 384),
                    g_dn[c, h].astype(f32).T,
                )
        start(store(n))
        if n == 2:
            load_dx.wait()
            wide[...] = low[...].astype(f32)
            load_y.wait()
            start([store_dx, store_y])
        if n == 4:
            wait(vec_loads)
            here = lax.axis_index("items")
            first = here * 96 - window_start(here)
            r_at = lax.broadcasted_iota(jnp.int32, (WINDOW, 96), 0)
            c_at = lax.broadcasted_iota(jnp.int32, (WINDOW, 96), 1)
            chosen = jnp.where(r_at - first == c_at, 1.0, 0.0)
            grad = jnp.dot(g_vec[...], chosen, preferred_element_type=f32, precision=lax.Precision.HIGHEST)
            new = adamw(b_vec[0], b_vec[1], b_vec[2], grad[:12], rates[4], decays[4])
            for k in range(3):
                b_vec[k] = new[k]
            start(vec_stores)

    for n in range(len(parts)):
        wait(store(n))
    wait([store_dx, store_y] + vec_stores)


def update(masters, firsts, seconds, gv, grads, y, dx):
    shapes = [jax.ShapeDtypeStruct(m.shape, f32) for m in masters]
    out = pl.pallas_call(
        update_kernel,
        out_shape=[jax.ShapeDtypeStruct(TOKENS, bf), jax.ShapeDtypeStruct(TOKENS, f32)] + shapes * 3,
        in_specs=[ANY] * 22,
        out_specs=[ANY] * 17,
        scratch_shapes=[
            pltpu.VMEM((3, 96, 3 * D), f32),
            pltpu.VMEM((3, 96, D), f32),
            pltpu.VMEM((3, 96, FF), f32),
            pltpu.VMEM((3, 384, D), f32),
            pltpu.VMEM((3, 12, 96), f32),
        ]
        + [pltpu.VMEM(g.shape, g.dtype) for g in (*grads, gv)]
        + [
            pltpu.VMEM(TOKENS, bf),
            pltpu.VMEM(TOKENS, bf),
            pltpu.VMEM(TOKENS, f32),
            pltpu.SemaphoreType.DMA((8, 3)),
            pltpu.SemaphoreType.DMA((8, 3)),
            pltpu.SemaphoreType.DMA((4,)),
            pltpu.SemaphoreType.DMA((4,)),
            pltpu.SemaphoreType.DMA((7,)),
        ],
        compiler_params=pltpu.CompilerParams(vmem_limit_bytes=63 * MIB),
    )(*masters, *firsts, *seconds, gv, *grads, y, dx)
    return out[0], out[1], [out[2 + 5 * k : 7 + 5 * k] for k in range(3)]


def plain_kernel(*refs):
    (xs, dys, counts, masks, w_qkv, w_o, w_up, w_dn, vecs, y, dx, gv, o_dn, o_up, o_o, o_q) = refs[:16]
    r = collections.namedtuple("Refs", list(LAYER_BUFFERS) + ["sem"])(*refs[16:])
    layer = Layer(r, Masks(counts, masks))
    loads = [(xs, r.x), (dys, r.dy), (w_qkv, r.wqkv), (w_o, r.wo), (w_up, r.wup), (w_dn, r.wdn), (vecs, r.vec)]

    def move(pairs):
        copies = [pltpu.make_async_copy(s, d, r.sem.at[n]) for n, (s, d) in enumerate(pairs)]
        for copy in copies:
            copy.start()
        for copy in copies:
            copy.wait()

    move(loads)
    layer.start()
    layer.spread_biases()
    for t in range(2):
        layer.norm_item(t)

    def part(n, _):
        layer.attend(n, {})
        return 0

    lax.fori_loop(0, 6, part, 0)
    layer.middle({})
    layer.feed({})
    move([(r.wup, o_up), (r.gdn, o_dn)])
    layer.turn(lambda k: k, lambda k, g: None, {})
    layer.out_grads()
    layer.attend_back({}, lambda k: k, lambda k, t: None)
    move(
        [(r.dy, y), (r.x, dx), (r.gv, gv), (r.wo, o_o)]
        + [(layer.qkv_grad(hq), o_q.at[hq]) for hq in range(3)]
    )


def plain_step(x, dy, counts, masks, weights):
    def swap(values):
        return lax.all_to_all(values, "blk", 0, 0, tiled=True)

    full = [lax.all_gather(w.astype(bf), "items", axis=0, tiled=True) for w in weights[:4]]
    vecs = lax.all_gather(weights[4].astype(bf), "items", axis=1, tiled=True).astype(f32)
    w_qkv = full[0].reshape(D, 3, 3, 256).transpose(2, 0, 1, 3).reshape(3, 4, 2, 2, 48, D)
    w_o = full[1].reshape(4, 2, 2, 48, D)
    w_up = full[2].reshape(D, OWNERS, CHUNKS, 128).transpose(2, 0, 1, 3).reshape(CHUNKS, 4, 2, 2, 48, WIDE)
    w_dn = full[3].reshape(OWNERS, CHUNKS, 128, D).transpose(1, 0, 2, 3).reshape(CHUNKS, 4, 2, 2, 64, D)
    vecs = jnp.pad(vecs, ((0, VROWS - vecs.shape[0]), (0, 0)))
    y, dx, gv, g_dn, g_up, g_o, g_q = pl.pallas_call(
        plain_kernel,
        out_shape=(
            jax.ShapeDtypeStruct(TOKENS, bf),
            jax.ShapeDtypeStruct(TOKENS, bf),
            jax.ShapeDtypeStruct((VROWS, D), f32),
            jax.ShapeDtypeStruct((CHUNKS, 4, 2, 2, 384, 128), bf),
            jax.ShapeDtypeStruct((CHUNKS, 4, 2, 2, 48, WIDE), bf),
            jax.ShapeDtypeStruct((4, 2, 2, 48, D), bf),
            jax.ShapeDtypeStruct((3, 4, 2, 2, 48, D), bf),
        ),
        in_specs=[ANY, ANY, SMEM, SMEM] + [ANY] * 5,
        out_specs=[ANY] * 7,
        scratch_shapes=[pltpu.VMEM(*spec) for spec in LAYER_BUFFERS.values()]
        + [pltpu.SemaphoreType.DMA((8,))],
        compiler_params=pltpu.CompilerParams(vmem_limit_bytes=63 * MIB),
    )(swap(x), swap(dy), counts, masks, w_qkv, w_o, w_up, w_dn, vecs)
    g_up = g_up.reshape(CHUNKS, D, OWNERS, 128).transpose(1, 2, 0, 3).reshape(D, FF)
    g_dn = g_dn.reshape(CHUNKS, OWNERS, D, 128).transpose(1, 0, 3, 2).reshape(FF, D)
    g_q = g_q.reshape(3, D, 3, 256).transpose(1, 2, 0, 3).reshape(D, 3 * D)

    def total(values, axis):
        share = lax.psum_scatter(values.astype(f32), "items", scatter_dimension=axis, tiled=True)
        return lax.psum(share, "blk")

    grads = [total(v, 0) for v in (g_q, g_o.reshape(D, D), g_up, g_dn)] + [total(gv[:12], 1)]
    return swap(y), swap(dx).astype(f32), grads


def body(block_input, block_cotangent, task_counts, group_mask, *states):
    masters, firsts, seconds = states[:5], states[5:10], states[10:]
    x = block_input.reshape(TOKENS)
    dy = block_cotangent.reshape(TOKENS)
    allowed = group_mask.transpose(1, 2, 0)
    if lax.axis_size("items") == OWNERS and lax.axis_size("blk") == GROUPS:
        y, dx, gv, *grads = step(x, dy, task_counts, allowed, masters)
        y, dx, new = update(masters, firsts, seconds, gv, grads, y, dx)
    else:
        y, dx, grads = plain_step(x, dy, task_counts, allowed, masters)
        parts = [
            adamw(masters[n], firsts[n], seconds[n], grads[n], rates[n], decays[n]) for n in range(5)
        ]
        new = [[part[k] for part in parts] for k in range(3)]
    return (y.reshape(block_input.shape), dx.reshape(block_input.shape), *new[0], *new[1], *new[2])


def solution(mesh):
    tokens = P("items", "blk", None, None)
    rows = P("items", None)
    state = (rows, rows, rows, rows, P(None, "items"))
    return jax.shard_map(
        body,
        mesh=mesh,
        in_specs=(tokens, tokens, P("items"), P("items", None, None)) + state * 3,
        out_specs=(tokens, tokens) + state * 3,
        check_vma=False,
    )
```
